512 devices in a mesh: dom: 512 (over x, z, y, core).
Axes of the slice: x: 4, y: 8, z: 8, core: 2. Of those that a mesh axis runs over, the one named last changes fastest.
Arguments:
- right_side: float32 [131072, 256], P('dom'), may hold values from -100 to 100
- noise_precision: bfloat16 [131072, 256], P('dom'), may hold values from 0.19921875 to 2
- degree: float32 [131072], P('dom'), as said below
- dependence: float32 [], replicated, may hold values from 0.5 to 0.95
- var_precision: float32 [256, 256], replicated, may hold values from -1 to 3, as said below
- local_tiles: float32 [1024, 2, 128, 128], P('dom'), may hold values from 0 to 0.06, as said below
- tile_cols: int32 [1024, 2], P('dom'), may hold values from 0 to 1, as said below
- tile_count: int32 [1024], P('dom'), may hold values from 1 to 2, as said below
- halo_tile: int32 [512, 4], P('dom'), may hold values from 0 to 1
- send_rows: int32 [512, 4, 64], P('dom'), may hold values from 0 to 127, as said below
- send_count: int32 [512, 4], P('dom'), may hold values from 0 to 64, as said below
- halo_weights: float32 [512, 4, 64, 128], P('dom'), may hold values from 0 to 0.06, as said below
Outputs:
- solution: float32 [131072, 256], P('dom')
The draws below stay inside these ranges and needn't reach their ends.
Inputs may be any that keep to these rules, and one draw needn't show every extreme that they name: `tile_cols`: for each row tile r, the first tile_count slots name distinct column tiles of the same partition in any order, one of them r itself; every named tile lies in r's aligned group of 2 row tiles; later slots name the other tiles of that group. `tile_count`: row tile s is named by row tile r exactly when r is named by s. Some row tile names 2 tiles. `local_tiles`: used slots hold the weights between the blocks of the row tile and of the named column tile; the tiles of the pairs (r, s) and (s, r) are transposes of each other, and no block is adjacent to itself. Unused slots hold arbitrary values. `send_rows`: for each partition and direction, the 64 slots name distinct blocks of that direction's border row tile. `send_count`: zero exactly where a partition has no neighbour in a direction, otherwise at least 16; some count equals 64. The weights are those of a symmetric W: for used slots, halo_weights[p, c, k, send_rows[p, c, l]] = halo_weights[q, c', l, send_rows[q, c', k]]; in a used slot, entries in blocks that are not among p's used send_rows of that direction are zero. Slots at or past the neighbour's send_count hold arbitrary values. `degree`: the sum of each block's row of W. `var_precision`: Symmetric.
All inputs are finite; a program needn't handle non-finite values.
Results may differ from the reference program's by a relative error of at most 0.0003.
Values sent between devices are 32-bit elements; how exact they have to be, the bound alone decides.
A program may use at most 64 MiB of HBM per device.

```python
import math
import jax
import jax.numpy as jnp
from jax import lax

VARIABLES = 256
BLOCKS_DEV = 256
TILE = 128
SLOTS = 64
GRID_W = 16
ITERS = 3
ROW_TILES = 2
TILE_SLOTS = 2
PARTITIONS = 512
BLOCKS = 131072
TILES = 1024


def grid_usable():
    domain_split = jnp.arange(PARTITIONS)
    column = domain_split % GRID_W
    return jnp.stack([column < GRID_W - 1, column > 0, domain_split + GRID_W < PARTITIONS, domain_split >= GRID_W], 1)


def local_structure(key):
    key = jax.random.fold_in(key, 11)
    key_busy, key_pick, key_score, key_value, key_order = jax.random.split(key, 5)
    busyness = jax.random.randint(key_busy, (PARTITIONS,), 0, 8, dtype=jnp.int32)
    chosen = jax.random.randint(key_pick, (), 0, PARTITIONS, dtype=jnp.int32)
    busyness = jnp.where(jnp.arange(PARTITIONS) == chosen, 7, busyness)
    scores = jax.random.randint(key_score, (PARTITIONS, ROW_TILES, ROW_TILES), 0, 4, dtype=jnp.int32)
    scores = scores + jnp.swapaxes(scores, 1, 2)
    row_ids = jnp.arange(ROW_TILES)
    step_ids = jnp.arange(TILE_SLOTS)
    partner = jnp.bitwise_xor(row_ids[:, None], step_ids[None, :])
    partner_all = jnp.broadcast_to(partner[None], (PARTITIONS, ROW_TILES, TILE_SLOTS))
    pair_score = jnp.take_along_axis(scores, partner_all, axis=2)
    present = (step_ids[None, None, :] == 0) | (pair_score < busyness[:, None, None])
    order_rank = jax.random.randint(key_order, (PARTITIONS, ROW_TILES, TILE_SLOTS), 0, 1024, dtype=jnp.int32)
    order_key = jnp.where(present, 0, 1) * (1024 * TILE_SLOTS) + order_rank * TILE_SLOTS + step_ids
    ordering = jnp.argsort(order_key, axis=-1)
    columns = jnp.take_along_axis(partner_all, ordering, axis=2).astype(jnp.int32)
    counted = jnp.sum(present.astype(jnp.int32), axis=-1)
    uniform_draw = jax.random.uniform(key_value, (PARTITIONS, ROW_TILES, TILE_SLOTS, TILE, TILE))
    mirrored = uniform_draw[:, partner, step_ids[None, :]]
    symmetric = 0.5 * (uniform_draw + jnp.swapaxes(mirrored, -1, -2))
    off_self = jnp.where(step_ids[:, None, None] == 0, 1.0 - jnp.eye(TILE), 1.0)
    weights = jnp.maximum(symmetric - 0.5, 0.0) * 0.12 * off_self[None, None]
    ordered = jnp.take_along_axis(weights, ordering[:, :, :, None, None], axis=2)
    leftward_aggregates = jnp.sum(weights * present[:, :, :, None, None].astype(jnp.float32), axis=(2, 4))
    return (columns.reshape(TILES, TILE_SLOTS), counted.reshape(TILES), ordered.reshape(TILES, TILE_SLOTS, TILE, TILE), leftward_aggregates)


def permuted_rows(single):
    return jax.random.permutation(single, TILE)[:SLOTS]


def boundary_structure(key):
    key = jax.random.fold_in(key, 23)
    key_tile, key_perm, key_count, key_pick, key_value, key_junk = jax.random.split(key, 6)
    usable = grid_usable()
    border_tile = jax.random.randint(key_tile, (PARTITIONS, 4), 0, ROW_TILES, dtype=jnp.int32)
    perm_keys = jax.random.split(key_perm, PARTITIONS * 4)
    chosen_rows = jax.vmap(permuted_rows)(perm_keys).reshape(PARTITIONS, 4, SLOTS).astype(jnp.int32)
    counts = jax.random.randint(key_count, (PARTITIONS, 4), SLOTS // 4, SLOTS + 1, dtype=jnp.int32)
    picked = jax.random.randint(key_pick, (), 0, PARTITIONS, dtype=jnp.int32)
    picked = picked - (picked % GRID_W == GRID_W - 1).astype(jnp.int32)
    forced = (jnp.arange(PARTITIONS)[:, None] == picked) & (jnp.arange(4)[None, :] == 0)
    counts = jnp.where(forced, SLOTS, counts) * usable.astype(jnp.int32)
    slot_ids = jnp.arange(SLOTS)
    onehot = (chosen_rows[..., None] == jnp.arange(TILE)).astype(jnp.float32)
    true_weights = jnp.zeros((PARTITIONS, 4, SLOTS, TILE), jnp.float32)
    value_keys = jax.random.split(key_value, 2)
    for number, (heading, facing, offset) in enumerate(((0, 1, 1), (2, 3, GRID_W))):
        adjoining_active = (slot_ids[None, :] < counts[:, heading, None]).astype(jnp.float32)
        far_live = (slot_ids[None, :] < jnp.roll(counts[:, facing], -offset, axis=0)[:, None]).astype(jnp.float32)
        uniform_draw = jax.random.uniform(value_keys[number], (PARTITIONS, SLOTS, SLOTS))
        pair_weights = jnp.maximum(uniform_draw - 0.5, 0.0) * 0.12 * far_live[:, :, None] * adjoining_active[:, None, :] * usable[:, heading, None, None].astype(jnp.float32)
        near_side = jnp.einsum('pkl,pla->pka', pair_weights, onehot[:, heading], precision=lax.Precision.HIGHEST)
        far_rows = jnp.roll(onehot[:, facing], -offset, axis=0)
        far_side = jnp.einsum('pkl,pkb->plb', pair_weights, far_rows, precision=lax.Precision.HIGHEST)
        true_weights = true_weights.at[:, heading].set(near_side)
        true_weights = true_weights.at[:, facing].set(jnp.roll(far_side, offset, axis=0))
    neighbour_count = jnp.stack([jnp.roll(counts[:, facing], -stride, axis=0) for facing, stride in ((1, 1), (0, -1), (3, GRID_W), (2, -GRID_W))], 1) * usable.astype(jnp.int32)
    spare = (slot_ids[None, None, :] >= neighbour_count[:, :, None]).astype(jnp.float32)
    filler = jax.random.uniform(key_junk, (PARTITIONS, 4, SLOTS, TILE), minval=0.0, maxval=0.06)
    halo_values = true_weights + filler * spare[:, :, :, None]
    leftward_aggregates = jnp.sum(true_weights, axis=2)
    submatrix_flag = (border_tile[:, :, None] == jnp.arange(ROW_TILES)).astype(jnp.float32)
    interface_accumulations = jnp.einsum('pnz,pnf->pzf', submatrix_flag, leftward_aggregates, precision=lax.Precision.HIGHEST)
    return (border_tile, chosen_rows, counts, halo_values, interface_accumulations)


def draw_local_tiles(key, part):
    return local_structure(key)[2]


def draw_tile_cols(key, part):
    return local_structure(key)[0]


def draw_tile_count(key, part):
    return local_structure(key)[1]


def draw_halo_tile(key, part):
    return boundary_structure(key)[0]


def draw_send_rows(key, part):
    return boundary_structure(key)[1]


def draw_send_count(key, part):
    return boundary_structure(key)[2]


def draw_halo_weights(key, part):
    return boundary_structure(key)[3]


def draw_degree(key, part):
    return (local_structure(key)[3] + boundary_structure(key)[4]).reshape(BLOCKS)


def draw_var_precision(key, part):
    key = jax.random.fold_in(key, 41)
    key_off, key_diag = jax.random.split(key)
    uniform_draw = jax.random.uniform(key_off, (VARIABLES, VARIABLES), minval=-1.0, maxval=1.0)
    coupling = (uniform_draw + uniform_draw.T) * (1.0 / VARIABLES) * (1.0 - jnp.eye(VARIABLES))
    diagonal = 2.0 + jax.random.uniform(key_diag, (VARIABLES,))
    return coupling + jnp.diag(diagonal)


def draw_right_side(key, part):
    key = jax.random.fold_in(key, 53)
    key_base, key_row, key_col = jax.random.split(key, 3)
    position = (jnp.arange(BLOCKS) // BLOCKS_DEV).astype(jnp.float32)
    ramp = position / (PARTITIONS - 1)
    row_scale = jnp.exp(jax.random.uniform(key_row, (BLOCKS, 1), minval=math.log(0.3), maxval=math.log(3.0)))
    rightward_factor = jnp.exp(jax.random.uniform(key_col, (1, VARIABLES), minval=math.log(0.3), maxval=math.log(3.0)))
    base = jax.random.truncated_normal(key_base, -4.0, 4.0, (BLOCKS, VARIABLES))
    growth = jnp.sqrt(1.0 + 2.0 * ramp)
    return base * growth[:, None] * row_scale * rightward_factor


def steps_of(rng, extent, cuts, least, top_value):
    gain = 1.0
    for dim, blocks in cuts:
        heights = jax.random.uniform(jax.random.fold_in(jax.random.fold_in(rng, 6), dim), (blocks,), jnp.float32, least / len(cuts), top_value / len(cuts))
        gain = gain * jnp.repeat(jnp.exp(heights), extent[dim] // blocks).reshape((-1,) + (1,) * (len(extent) - 1 - dim))
    return gain


def setup_inputs(seed: int = 0) -> dict:
    seeds = jax.random.split(jax.random.key(seed), 13)
    right_side = draw_right_side(jax.random.fold_in(seeds[12], 71), 0)
    noise_precision = jnp.clip(jnp.exp(math.log(2.0) - 2.306499 * jax.random.uniform(seeds[1], (BLOCKS, VARIABLES), jnp.float32) ** steps_of(seeds[1], (BLOCKS, VARIABLES), ((0, 512),), -0.2, 0.2)), 0.19921875, 2.0).astype(jnp.bfloat16)
    degree = draw_degree(jax.random.fold_in(seeds[12], 71), 0)
    dependence = jnp.clip(jax.random.uniform(seeds[3], (), jnp.float32, 0.5, 0.95), 0.5, 0.95)
    var_precision = draw_var_precision(jax.random.fold_in(seeds[12], 71), 0)
    local_tiles = draw_local_tiles(jax.random.fold_in(seeds[12], 71), 0)
    tile_cols = draw_tile_cols(jax.random.fold_in(seeds[12], 71), 0)
    tile_count = draw_tile_count(jax.random.fold_in(seeds[12], 71), 0)
    halo_tile = draw_halo_tile(jax.random.fold_in(seeds[12], 71), 0)
    send_rows = draw_send_rows(jax.random.fold_in(seeds[12], 71), 0)
    send_count = draw_send_count(jax.random.fold_in(seeds[12], 71), 0)
    halo_weights = draw_halo_weights(jax.random.fold_in(seeds[12], 71), 0)
    return {"right_side": right_side, "noise_precision": noise_precision, "degree": degree, "dependence": dependence, "var_precision": var_precision, "local_tiles": local_tiles, "tile_cols": tile_cols, "tile_count": tile_count, "halo_tile": halo_tile, "send_rows": send_rows, "send_count": send_count, "halo_weights": halo_weights}


highest_precision = lax.Precision.HIGHEST


def neighbour_usable(dtype):
    domain_split = jnp.arange(PARTITIONS)
    column = domain_split % GRID_W
    neighbours = jnp.stack([column < GRID_W - 1, column > 0, domain_split + GRID_W < PARTITIONS, domain_split >= GRID_W], 1)
    return neighbours.astype(dtype)


def local_part(pieces):
    tile_set, columns, counted, as_tiles = pieces
    in_use = (jnp.arange(TILE_SLOTS)[None, :] < counted[:, None]).astype(as_tiles.dtype)
    picked = as_tiles[columns]
    return jnp.einsum("rjab,rjbv->rav", tile_set * in_use[:, :, None, None], picked, precision=highest_precision)


def pick_rows(block_rows, indices):
    return block_rows[indices]


def apply_operator(vector, degree, dependence, var_precision, noise_wide, local_tiles, tile_cols, tile_count, halo_tile, send_rows, send_count, halo_weights):
    as_tiles = vector.reshape(PARTITIONS, ROW_TILES, TILE, VARIABLES)
    within = lax.map(local_part, (local_tiles.reshape(PARTITIONS, ROW_TILES, TILE_SLOTS, TILE, TILE), tile_cols.reshape(PARTITIONS, ROW_TILES, TILE_SLOTS), tile_count.reshape(PARTITIONS, ROW_TILES), as_tiles))
    by_part = vector.reshape(PARTITIONS, BLOCKS_DEV, VARIABLES)
    indices = halo_tile[:, :, None] * TILE + send_rows
    packed = jax.vmap(pick_rows)(by_part, indices)
    in_use = (jnp.arange(SLOTS)[None, None, :] < send_count[:, :, None]).astype(vector.dtype)
    packed = packed * in_use[:, :, :, None]
    usable = neighbour_usable(vector.dtype)
    arrived = []
    for heading, (facing, stride) in enumerate(((1, 1), (0, -1), (3, GRID_W), (2, -GRID_W))):
        arrived.append(jnp.roll(packed[:, facing], -stride, axis=0) * usable[:, heading, None, None])
    arrived = jnp.stack(arrived, 1)
    boundary_terms = jnp.einsum("pcka,pckv->pcav", halo_weights, arrived, precision=highest_precision)
    placement_choice = (halo_tile[:, :, None] == jnp.arange(ROW_TILES)[None, None, :]).astype(vector.dtype)
    boundary_edge = jnp.einsum("lfu,lfbq->lubq", placement_choice, boundary_terms, precision=highest_precision)
    coupled = (within + boundary_edge).reshape(BLOCKS, VARIABLES)
    interim = degree[:, None] * vector - dependence * coupled
    return jnp.dot(interim, var_precision, precision=highest_precision, preferred_element_type=jnp.float32) + noise_wide * vector


def reference(right_side, noise_precision, degree, dependence, var_precision, local_tiles, tile_cols, tile_count, halo_tile, send_rows, send_count, halo_weights):
    noise_wide = noise_precision.astype(jnp.float32)
    solution = jnp.zeros_like(right_side)
    residual = right_side
    direction = right_side
    norm_now = jnp.sum(residual * residual)
    for iteration in range(ITERS):
        image = apply_operator(direction, degree, dependence, var_precision, noise_wide, local_tiles, tile_cols, tile_count, halo_tile, send_rows, send_count, halo_weights)
        step_size = norm_now / jnp.sum(direction * image)
        solution = solution + step_size * direction
        residual = residual - step_size * image
        norm_next = jnp.sum(residual * residual)
        direction = residual + (norm_next / norm_now) * direction
        norm_now = norm_next
    return solution
```

```python
import functools

import jax
import jax.numpy as jnp
from jax import lax
from jax.experimental import pallas as pl
from jax.experimental.pallas import tpu as pltpu
from jax.sharding import PartitionSpec as P

MESH = pl.DeviceIdType.MESH
GRID_W = 16
ITERS = 3
OFFSETS = (1, -1, GRID_W, -GRID_W)
REVERSE = (1, 0, 3, 2)
STAGES = ((1, 16), (16, 8), (128, 4))
F32 = jnp.float32
BF16 = jnp.bfloat16


def split(value):
    high = value.astype(BF16)
    low = (value - high.astype(F32)).astype(BF16)
    return high, low


def as_left(value):
    high, low = split(value)
    return jnp.concatenate([high, low, high], axis=1)


def as_right(value):
    high, low = split(value)
    return jnp.concatenate([high, low, high], axis=0)


def keep_left(ref, value):
    high, low = split(value)
    n = value.shape[1]
    ref[:, 0:n] = high
    ref[:, n : 2 * n] = high
    ref[:, 2 * n : 3 * n] = low


def keep_right(ref, value):
    high, low = split(value)
    n = value.shape[0]
    ref[0:n, :] = high
    ref[n : 2 * n, :] = high
    ref[2 * n : 3 * n, :] = low


def dot(a, b):
    return jnp.dot(a, b, preferred_element_type=F32)


def fold(value):
    rows, lanes = value.shape
    tile = jnp.sum(value.reshape(rows // 8, 8, lanes), axis=0)
    tile = tile[:, 0:128] + tile[:, 128:256]
    return jnp.sum(tile, axis=0, keepdims=True)


def total_of(row):
    return jnp.sum(row, axis=1, keepdims=True)


def kernel(
    dependence_ref,
    tile_cols_ref,
    tile_count_ref,
    halo_tile_ref,
    send_count_ref,
    right_hbm,
    noise_hbm,
    degree_hbm,
    var_hbm,
    tiles_hbm,
    rows_hbm,
    halo_hbm,
    out_ref,
    right_ref,
    noise_ref,
    degree_ref,
    var_ref,
    tiles_ref,
    rows_ref,
    halo_ref,
    var_cat,
    local_cat,
    halo_cat,
    scatter,
    basis,
    sent,
    received,
    sums,
    load_sem,
    send_sem,
    recv_sem,
    sum_send_sem,
    sum_recv_sem,
):
    me = lax.axis_index("dom")
    loads = [
        pltpu.make_async_copy(src, dst, load_sem.at[i])
        for i, (src, dst) in enumerate(
            (
                (var_hbm, var_ref),
                (right_hbm, right_ref),
                (halo_hbm, halo_ref),
                (tiles_hbm, tiles_ref),
                (rows_hbm, rows_ref),
                (degree_hbm, degree_ref),
                (noise_hbm, noise_ref),
            )
        )
    ]
    for load in loads:
        load.start()

    column = lax.rem(me, GRID_W)
    line = me // GRID_W
    usable = (column < GRID_W - 1, column > 0, line < 512 // GRID_W - 1, line > 0)

    def partners(stride, size):
        place = lax.rem(me // stride, size)
        return [me + (lax.rem(place + j, size) - place) * stride for j in range(1, size)]

    barrier = pltpu.get_barrier_semaphore()
    greeted = 0
    for stride, size in STAGES:
        for partner in partners(stride, size):
            pl.semaphore_signal(barrier, inc=1, device_id=(partner,), device_id_type=MESH)
            greeted += 1
    for c in range(4):

        @pl.when(usable[c])
        def _():
            pl.semaphore_signal(barrier, inc=1, device_id=(me + OFFSETS[c],), device_id_type=MESH)

    for c in range(4):

        @pl.when(jnp.logical_not(usable[c]))
        def _():
            for k in range(ITERS):
                received[k, 64 * c : 64 * c + 64, :] = jnp.zeros((64, 256), F32)

    loads[0].wait()
    keep_right(var_cat, var_ref[...])
    loads[1].wait()
    loads[2].wait()
    for c in range(4):
        tile = halo_tile_ref[0, c]
        weights = halo_ref[0, c]
        block = jnp.concatenate(
            [jnp.where(tile == r, weights, jnp.zeros_like(weights)) for r in range(2)], axis=1
        )
        keep_left(halo_cat.at[64 * c : 64 * c + 64, :], block)

    field = right_ref[...]
    mapped = dot(as_left(field), var_cat[...])
    mapped_cat = as_right(mapped)
    outgoing = dot(halo_cat[...], mapped_cat)

    pl.semaphore_wait(barrier, greeted + sum(u.astype(jnp.int32) for u in usable))

    def copies(k):
        return [
            pltpu.make_async_remote_copy(
                src_ref=sent.at[k, 64 * c : 64 * c + 64, :],
                dst_ref=received.at[k, 64 * REVERSE[c] : 64 * REVERSE[c] + 64, :],
                send_sem=send_sem.at[k, c],
                recv_sem=recv_sem.at[k, REVERSE[c]],
                device_id=(me + OFFSETS[c],),
                device_id_type=MESH,
            )
            for c in range(4)
        ]

    def arrivals(k):
        return [
            pltpu.make_async_remote_copy(
                src_ref=sent.at[k, 64 * c : 64 * c + 64, :],
                dst_ref=received.at[k, 64 * c : 64 * c + 64, :],
                send_sem=send_sem.at[k, c],
                recv_sem=recv_sem.at[k, c],
                device_id=(me + OFFSETS[c],),
                device_id_type=MESH,
            )
            for c in range(4)
        ]

    def start(k, value):
        sent[k] = value
        for c in (2, 3, 0, 1):
            pl.when(usable[c])(copies(k)[c].start)

    def finish(k):
        for c in (0, 1, 2, 3):
            pl.when(usable[c])(arrivals(k)[c].wait_recv)

    start(0, outgoing)

    dependence = dependence_ref[0]
    loads[3].wait()
    loads[5].wait()
    on_diagonal = lax.broadcasted_iota(jnp.int32, (256, 256), 0) == lax.broadcasted_iota(
        jnp.int32, (256, 256), 1
    )
    diagonal = jnp.where(on_diagonal, degree_ref[...], 0.0)
    for r in range(2):
        row = []
        for s in range(2):
            block = jnp.zeros((128, 128), F32)
            for j in range(2):
                used = jnp.logical_and(tile_cols_ref[r, j] == s, tile_count_ref[r] > j)
                block = jnp.where(used, tiles_ref[r, j], block)
            row.append(block)
        block_row = diagonal[128 * r : 128 * r + 128] - dependence * jnp.concatenate(row, axis=1)
        keep_left(local_cat.at[128 * r : 128 * r + 128, :], block_row)
    loads[4].wait()
    places = []
    slot = lax.broadcasted_iota(jnp.int32, (1, 64), 1)
    for c in range(4):
        place = rows_ref[0, c : c + 1, :] + halo_tile_ref[0, c] * 128
        places.append(jnp.where(slot < send_count_ref[0, c], place, -1))
    places = jnp.concatenate(places, axis=1)
    hot = lax.broadcasted_iota(jnp.int32, (256, 256), 0) == places
    hot = jnp.where(hot, 1.0, 0.0).astype(BF16)
    scatter[:, 0:256] = hot
    scatter[:, 256:512] = hot
    loads[6].wait()

    moments = [fold(field * field)]
    basis[0] = field
    for k in range(ITERS):
        near = dot(local_cat[...], mapped_cat) + noise_ref[...].astype(F32) * field
        finish(k)
        far = dot(scatter[...], jnp.concatenate(split(received[k]), axis=0))
        image = near - dependence * far
        moments.append(fold(field * image))
        if k + 1 < ITERS:
            moments.append(fold(image * image))
            field = image
            basis[k + 1] = field
            mapped = dot(as_left(field), var_cat[...])
            mapped_cat = as_right(mapped)
            start(k + 1, dot(halo_cat[...], mapped_cat))

    sums[0, 0] = jnp.concatenate(moments + [jnp.zeros((2, 128), F32)], axis=0)
    pending = []
    for n, (stride, size) in enumerate(STAGES):
        moves = [
            pltpu.make_async_remote_copy(
                src_ref=sums.at[n, 0],
                dst_ref=sums.at[n, size - 1 - j],
                send_sem=sum_send_sem.at[n],
                recv_sem=sum_recv_sem.at[n],
                device_id=(partner,),
                device_id_type=MESH,
            )
            for j, partner in enumerate(partners(stride, size))
        ]
        for move in moves:
            move.start()
        whole = pltpu.make_async_remote_copy(
            src_ref=sums.at[n, 1:size],
            dst_ref=sums.at[n, 1:size],
            send_sem=sum_send_sem.at[n],
            recv_sem=sum_recv_sem.at[n],
            device_id=(me,),
            device_id_type=MESH,
        )
        whole.wait_recv()
        total = sums[n, 0]
        for j in range(1, size):
            total = total + sums[n, j]
        if n + 1 < len(STAGES):
            sums[n + 1, 0] = total
        pending.append(whole)

    m = [total[k : k + 1, :] for k in range(6)]
    rr0 = total_of(m[0])
    a0 = rr0 / total_of(m[1])
    rr1 = total_of(m[0] - 2.0 * a0 * m[1] + a0 * a0 * m[2])
    g0 = 1.0 + rr1 / rr0
    g1 = -a0
    a1 = rr1 / total_of(g0 * g0 * m[1] + 2.0 * g0 * g1 * m[2] + g1 * g1 * m[3])
    e1 = -a0 - a1 * g0
    e2 = -a1 * g1
    rr2 = total_of(
        m[0] + 2.0 * e1 * m[1] + (e1 * e1 + 2.0 * e2) * m[2] + 2.0 * e1 * e2 * m[3] + e2 * e2 * m[4]
    )
    b1 = rr2 / rr1
    f0 = 1.0 + b1 * g0
    f1 = e1 + b1 * g1
    f2 = e2
    a2 = rr2 / total_of(
        f0 * f0 * m[1]
        + 2.0 * f0 * f1 * m[2]
        + (f1 * f1 + 2.0 * f0 * f2) * m[3]
        + 2.0 * f1 * f2 * m[4]
        + f2 * f2 * m[5]
    )
    c0 = a0 + a1 * g0 + a2 * f0
    c1 = a1 * g1 + a2 * f1
    c2 = a2 * f2
    out_ref[...] = c0 * basis[0] + c1 * basis[1] + c2 * basis[2]

    for move in pending:
        move.wait_send()
    for k in range(ITERS):
        for c in range(4):
            pl.when(usable[c])(copies(k)[c].wait_send)


def local(
    right_side,
    noise_precision,
    degree,
    dependence,
    var_precision,
    local_tiles,
    tile_cols,
    tile_count,
    halo_tile,
    send_rows,
    send_count,
    halo_weights,
):
    smem = pl.BlockSpec(memory_space=pltpu.SMEM)
    hbm = pl.BlockSpec(memory_space=pl.ANY)
    return pl.pallas_call(
        kernel,
        out_shape=jax.ShapeDtypeStruct((256, 256), F32),
        in_specs=[smem] * 5 + [hbm] * 7,
        out_specs=pl.BlockSpec(memory_space=pltpu.VMEM),
        scratch_shapes=[
            pltpu.VMEM((256, 256), F32),
            pltpu.VMEM((256, 256), BF16),
            pltpu.VMEM((1, 256), F32),
            pltpu.VMEM((256, 256), F32),
            pltpu.VMEM((2, 2, 128, 128), F32),
            pltpu.VMEM((1, 4, 64), jnp.int32),
            pltpu.VMEM((1, 4, 64, 128), F32),
            pltpu.VMEM((768, 256), BF16),
            pltpu.VMEM((256, 768), BF16),
            pltpu.VMEM((256, 768), BF16),
            pltpu.VMEM((256, 512), BF16),
            pltpu.VMEM((ITERS, 256, 256), F32),
            pltpu.VMEM((ITERS, 256, 256), F32),
            pltpu.VMEM((ITERS, 256, 256), F32),
            pltpu.VMEM((len(STAGES), max(s for _, s in STAGES), 8, 128), F32),
            pltpu.SemaphoreType.DMA((7,)),
            pltpu.SemaphoreType.DMA((ITERS, 4)),
            pltpu.SemaphoreType.DMA((ITERS, 4)),
            pltpu.SemaphoreType.DMA((len(STAGES),)),
            pltpu.SemaphoreType.DMA((len(STAGES),)),
        ],
        compiler_params=pltpu.CompilerParams(
            collective_id=0, has_side_effects=True, vmem_limit_bytes=48 * 1024 * 1024
        ),
        name="conjugate_gradient",
    )(
        dependence.reshape(1),
        tile_cols,
        tile_count,
        halo_tile,
        send_count,
        right_side,
        noise_precision,
        degree.reshape(1, 256),
        var_precision,
        local_tiles,
        send_rows,
        halo_weights,
    )


def solution(mesh):
    placed = (
        P("dom", None),
        P("dom", None),
        P("dom"),
        P(),
        P(),
        P("dom", None, None, None),
        P("dom", None),
        P("dom"),
        P("dom", None),
        P("dom", None, None),
        P("dom", None),
        P("dom", None, None, None),
    )
    return jax.shard_map(
        local, mesh=mesh, in_specs=placed, out_specs=P("dom", None), check_vma=False
    )
```

```python
import functools

import jax
import jax.numpy as jnp
from jax import lax
from jax.experimental import pallas as pl
from jax.experimental.pallas import tpu as pltpu
from jax.sharding import PartitionSpec as P

MESH = pl.DeviceIdType.MESH
GRID_W = 16
OFFSETS = (1, -1, GRID_W, -GRID_W)
REVERSE = (1, 0, 3, 2)
STAGES = ((1, 16), (16, 32))
F32 = jnp.float32
BF16 = jnp.bfloat16


def ring(distance, size):
    return min(distance, size - distance)


def farthest_first(stride, size):
    def hops(mask):
        if stride == 1:
            return max(ring(abs((a ^ mask) // 2 - a // 2), size // 2) for a in range(size))
        return max(
            ring(abs((a ^ mask) % 8 - a % 8), 8) + ring(abs((a ^ mask) // 8 - a // 8), size // 8)
            for a in range(size)
        )

    return sorted(range(1, size), key=lambda mask: -hops(mask))


def split(value):
    high = value.astype(BF16)
    low = (value - high.astype(F32)).astype(BF16)
    return high, low


def as_left(value):
    high, low = split(value)
    return jnp.concatenate([high, low, high], axis=1)


def as_right(value):
    high, low = split(value)
    return jnp.concatenate([high, low, high], axis=0)


def keep_left(ref, value):
    high, low = split(value)
    n = value.shape[1]
    ref[:, 0:n] = high
    ref[:, n : 2 * n] = high
    ref[:, 2 * n : 3 * n] = low


def keep_right(ref, value):
    high, low = split(value)
    n = value.shape[0]
    ref[0:n, :] = high
    ref[n : 2 * n, :] = high
    ref[2 * n : 3 * n, :] = low


def dot(a, b):
    return jnp.dot(a, b, preferred_element_type=F32)


def fold(value):
    rows, lanes = value.shape
    tile = jnp.sum(value.reshape(rows // 8, 8, lanes), axis=0)
    tile = tile[:, 0:128] + tile[:, 128:256]
    return jnp.sum(tile, axis=0, keepdims=True)


def total_of(row):
    return jnp.sum(row, axis=1, keepdims=True)


def kernel(
    right_hbm,
    noise_hbm,
    degree_hbm,
    dependence_ref,
    var_hbm,
    tiles_hbm,
    cols_hbm,
    count_hbm,
    border_hbm,
    rows_hbm,
    live_hbm,
    halo_hbm,
    out_ref,
    right_ref,
    noise_ref,
    degree_ref,
    var_ref,
    tiles_ref,
    cols_ref,
    count_ref,
    border_ref,
    rows_ref,
    live_ref,
    halo_ref,
    var_cat,
    local_cat,
    halo_cat,
    hop_cat,
    scatter,
    gather,
    basis,
    sent,
    received,
    sums_a,
    sums_b,
    load_sem,
    send_sem,
    recv_sem,
    sum_send_sem,
    sum_recv_sem,
):
    me = lax.axis_index("dom")
    pairs = {
        "right": (right_hbm, right_ref),
        "noise": (noise_hbm, noise_ref),
        "degree": (degree_hbm, degree_ref),
        "var": (var_hbm, var_ref),
        "tiles": (tiles_hbm, tiles_ref),
        "cols": (cols_hbm, cols_ref),
        "count": (count_hbm, count_ref),
        "border": (border_hbm, border_ref),
        "rows": (rows_hbm, rows_ref),
        "live": (live_hbm, live_ref),
        "halo": (halo_hbm, halo_ref),
    }
    loads = {
        name: pltpu.make_async_copy(src, dst, load_sem.at[i])
        for i, (name, (src, dst)) in enumerate(pairs.items())
    }
    for name in (
        "border",
        "halo",
        "right",
        "var",
        "live",
        "rows",
        "tiles",
        "cols",
        "count",
        "degree",
        "noise",
    ):
        loads[name].start()

    column = jnp.bitwise_and(me, GRID_W - 1)
    line = jnp.right_shift(me, 4)
    usable = (column < GRID_W - 1, column > 0, line < 512 // GRID_W - 1, line > 0)

    odd = jnp.bitwise_and(me, 1)

    def partners(stride, size):
        return [(j, jnp.bitwise_xor(me, j * stride)) for j in farthest_first(stride, size)]

    barrier = pltpu.get_barrier_semaphore()
    for c in range(4):

        @pl.when(usable[c])
        def _():
            pl.semaphore_signal(barrier, inc=1, device_id=(me + OFFSETS[c],), device_id_type=MESH)

    greeted = 0
    for stride, size in STAGES:
        for _, partner in partners(stride, size):
            pl.semaphore_signal(barrier, inc=1, device_id=(partner,), device_id_type=MESH)
            greeted += 1

    for c in range(4):

        @pl.when(jnp.logical_not(usable[c]))
        def _():
            for k in range(2):
                received[k, 64 * c : 64 * c + 64, :] = jnp.zeros((64, 256), F32)

    loads["border"].wait()
    loads["halo"].wait()
    for c in range(4):
        tile = border_ref[0, c]
        weights = halo_ref[0, c]
        block = jnp.concatenate(
            [jnp.where(tile == r, weights, jnp.zeros_like(weights)) for r in range(2)], axis=1
        )
        keep_left(halo_cat.at[64 * c : 64 * c + 64, :], block)
    loads["right"].wait()
    field = right_ref[...]
    field_cat = as_right(field)
    outgoing = dot(halo_cat[...], field_cat)

    pl.semaphore_wait(barrier, greeted + sum(u.astype(jnp.int32) for u in usable))

    def copy(k, c, to):
        return pltpu.make_async_remote_copy(
            src_ref=sent.at[k, 64 * c : 64 * c + 64, :],
            dst_ref=received.at[k, 64 * to : 64 * to + 64, :],
            send_sem=send_sem.at[k, c],
            recv_sem=recv_sem.at[k, to],
            device_id=(me + OFFSETS[c],),
            device_id_type=MESH,
        )

    def start(k):
        for c in (2, 3, 0, 1):
            pl.when(usable[c])(copy(k, c, REVERSE[c]).start)

    def finish(k):
        for c in (0, 1, 3, 2):
            pl.when(usable[c])(copy(k, c, c).wait_recv)

    def last(i, device):
        return pltpu.make_async_remote_copy(
            src_ref=sent.at[2, 64 * i : 64 * i + 64, :],
            dst_ref=received.at[2, 64 * i : 64 * i + 64, :],
            send_sem=send_sem.at[2, i],
            recv_sem=recv_sem.at[2, i],
            device_id=(device,),
            device_id_type=MESH,
        )

    across = GRID_W * (2 * odd - 1)
    down, up = usable[3], usable[2]
    even = odd == 0
    crosses = jnp.logical_or(jnp.logical_and(even, down), jnp.logical_and(odd == 1, up))
    crossed = jnp.logical_or(jnp.logical_and(even, up), jnp.logical_and(odd == 1, down))
    from_slots = pl.ds(pl.multiple_of(192 - 64 * odd, 64), 64)
    to_slots = pl.ds(pl.multiple_of(128 + 64 * odd, 64), 64)

    @pl.when(jnp.logical_not(usable[0]))
    def _():
        received[2, 0:64, :] = jnp.zeros((64, 256), F32)

    @pl.when(jnp.logical_not(crossed))
    def _():
        received[2, 64:128, :] = jnp.zeros((64, 256), F32)

    sent[0] = outgoing
    start(0)

    loads["var"].wait()
    keep_right(var_cat, var_ref[...])

    loads["live"].wait()
    loads["rows"].wait()
    places = []
    slot = lax.broadcasted_iota(jnp.int32, (1, 64), 1)
    for c in range(4):
        place = rows_ref[0, c : c + 1, :] + border_ref[0, c] * 128
        places.append(jnp.where(slot < live_ref[0, c], place, -1))
    places = jnp.concatenate(places, axis=1)
    hot = lax.broadcasted_iota(jnp.int32, (256, 256), 0) == places
    hot_wide = jnp.where(hot, 1.0, 0.0)
    hot = hot_wide.astype(BF16)
    scatter[:, 0:256] = hot
    scatter[:, 256:512] = hot

    for name in ("tiles", "cols", "count", "degree"):
        loads[name].wait()
    dependence = dependence_ref[0]
    on_diagonal = lax.broadcasted_iota(jnp.int32, (256, 256), 0) == lax.broadcasted_iota(
        jnp.int32, (256, 256), 1
    )
    diagonal = jnp.where(on_diagonal, degree_ref[...], 0.0)
    for r in range(2):
        row = []
        for s in range(2):
            block = jnp.zeros((128, 128), F32)
            for j in range(2):
                used = jnp.logical_and(cols_ref[r, j] == s, count_ref[r] > j)
                block = jnp.where(used, tiles_ref[r, j], block)
            row.append(block)
        block_row = diagonal[128 * r : 128 * r + 128] - dependence * jnp.concatenate(row, axis=1)
        keep_left(local_cat.at[128 * r : 128 * r + 128, :], block_row)
    loads["noise"].wait()
    noise = noise_ref[...].astype(F32)

    hop_cat[:, 0:256] = dot(halo_cat[:, 0:256], hot).astype(BF16)
    hop_cat[:, 256:512] = hop_cat[:, 0:256]
    hop_cat[:, 512:768] = dot(halo_cat[:, 512:768], hot).astype(BF16)
    gather[...] = hot_wide.T.astype(BF16)

    basis[0] = field
    moments = [fold(field * field)]
    for k in range(2):
        near = dot(as_left(dot(local_cat[...], field_cat)), var_cat[...]) + noise * field
        next_near = dot(halo_cat[...], as_right(near))
        finish(k)
        arrived = dot(as_left(received[k]), var_cat[...])
        arrived_cat = as_right(arrived)
        if k == 0:
            sent[1] = next_near - dependence * dot(hop_cat[...], arrived_cat)
            start(1)
        else:
            hop = jnp.concatenate([hop_cat[64:128, :], hop_cat[from_slots, :]], axis=0)
            crossing = jnp.where(even, next_near[192:256], next_near[128:192])
            outgoing = jnp.concatenate([next_near[64:128], crossing], axis=0)
            sent[2, 0:128, :] = outgoing - dependence * dot(hop, arrived_cat)
            pl.when(crosses)(last(1, me + across).start)
            pl.when(usable[1])(last(0, me - 1).start)
        image = near - dependence * dot(scatter[...], arrived_cat[0:512])
        moments.append(fold(field * image))
        moments.append(fold(image * image))
        field = image
        field_cat = as_right(field)
        basis[k + 1] = field

    mapped = dot(as_left(field), var_cat[...])
    near = fold(dot(local_cat[...], field_cat) * mapped + noise * (field * field))
    high, low = split(mapped)
    picks = jnp.concatenate([gather[0:64, :], gather[to_slots, :]], axis=0)
    picked = dot(picks, high) + dot(picks, low)
    picked = (-2.0 * dependence) * picked
    lane = lax.broadcasted_iota(jnp.int32, (8, 128), 1)
    line_of = lax.broadcasted_iota(jnp.int32, (8, 128), 0)

    def pack(rows):
        tile = jnp.concatenate(rows, axis=0)
        for shift in (64, 32, 16):
            tile = tile + pltpu.roll(tile, shift, 1)
        return jnp.sum(jnp.where(lane // 16 == line_of, tile, 0.0), axis=0, keepdims=True)

    early = pack(moments + [near, jnp.zeros((2, 128), F32)])
    pl.when(usable[0])(last(0, me + 1).wait_recv)
    pl.when(crossed)(last(1, me - across).wait_recv)
    cross = fold(picked * received[2, 0:128, :])
    for shift in (64, 32, 16):
        cross = cross + pltpu.roll(cross, shift, 1)
    total = early + jnp.where(lane[0:1] // 16 == 5, cross, 0.0)

    pending = []
    for n, ((stride, size), sums) in enumerate(zip(STAGES, (sums_a, sums_b))):
        sums[0:1, :] = total
        for j, partner in partners(stride, size):
            pltpu.make_async_remote_copy(
                src_ref=sums.at[0:1, :],
                dst_ref=sums.at[j : j + 1, :],
                send_sem=sum_send_sem.at[n],
                recv_sem=sum_recv_sem.at[n],
                device_id=(partner,),
                device_id_type=MESH,
            ).start()
        whole = pltpu.make_async_remote_copy(
            src_ref=sums.at[1:size, :],
            dst_ref=sums.at[1:size, :],
            send_sem=sum_send_sem.at[n],
            recv_sem=sum_recv_sem.at[n],
            device_id=(me,),
            device_id_type=MESH,
        )
        whole.wait_recv()
        total = jnp.sum(sums[...], axis=0, keepdims=True)
        pending.append(whole)

    m = [
        jnp.where(lane[0:1] < 16, total if k == 0 else pltpu.roll(total, 128 - 16 * k, 1), 0.0)
        for k in range(6)
    ]
    rr0 = total_of(m[0])
    a0 = rr0 / total_of(m[1])
    rr1 = total_of(m[0] - 2.0 * a0 * m[1] + a0 * a0 * m[2])
    g0 = 1.0 + rr1 / rr0
    g1 = -a0
    a1 = rr1 / total_of(g0 * g0 * m[1] + 2.0 * g0 * g1 * m[2] + g1 * g1 * m[3])
    e1 = -a0 - a1 * g0
    e2 = -a1 * g1
    rr2 = total_of(
        m[0] + 2.0 * e1 * m[1] + (e1 * e1 + 2.0 * e2) * m[2] + 2.0 * e1 * e2 * m[3] + e2 * e2 * m[4]
    )
    b1 = rr2 / rr1
    f0 = 1.0 + b1 * g0
    f1 = e1 + b1 * g1
    f2 = e2
    a2 = rr2 / total_of(
        f0 * f0 * m[1]
        + 2.0 * f0 * f1 * m[2]
        + (f1 * f1 + 2.0 * f0 * f2) * m[3]
        + 2.0 * f1 * f2 * m[4]
        + f2 * f2 * m[5]
    )
    c0 = a0 + a1 * g0 + a2 * f0
    c1 = a1 * g1 + a2 * f1
    c2 = a2 * f2
    out_ref[...] = c0 * basis[0] + c1 * basis[1] + c2 * basis[2]

    for whole in pending:
        whole.wait_send()
    for k in range(2):
        for c in range(4):
            pl.when(usable[c])(copy(k, c, REVERSE[c]).wait_send)
    pl.when(usable[1])(last(0, me - 1).wait_send)
    pl.when(crosses)(last(1, me + across).wait_send)


def local(
    right_side,
    noise_precision,
    degree,
    dependence,
    var_precision,
    local_tiles,
    tile_cols,
    tile_count,
    halo_tile,
    send_rows,
    send_count,
    halo_weights,
):
    operands = (
        right_side,
        noise_precision,
        degree.reshape(1, 256),
        dependence.reshape(1),
        var_precision,
        local_tiles,
        tile_cols,
        tile_count,
        halo_tile,
        send_rows,
        send_count,
        halo_weights,
    )
    operands = [
        x if x.size == 1 else pltpu.with_memory_space_constraint(x, pltpu.HBM) for x in operands
    ]
    specs = [pl.BlockSpec(memory_space=pltpu.SMEM if x.size == 1 else pltpu.HBM) for x in operands]
    held = (
        pltpu.VMEM((256, 256), F32),
        pltpu.VMEM((256, 256), BF16),
        pltpu.VMEM((1, 256), F32),
        pltpu.VMEM((256, 256), F32),
        pltpu.VMEM((2, 2, 128, 128), F32),
        pltpu.SMEM((2, 2), jnp.int32),
        pltpu.SMEM((2,), jnp.int32),
        pltpu.SMEM((1, 4), jnp.int32),
        pltpu.VMEM((1, 4, 64), jnp.int32),
        pltpu.SMEM((1, 4), jnp.int32),
        pltpu.VMEM((1, 4, 64, 128), F32),
    )
    return pl.pallas_call(
        kernel,
        out_shape=pltpu.VMEM((256, 256), F32),
        in_specs=specs,
        out_specs=pl.BlockSpec(memory_space=pltpu.VMEM),
        scratch_shapes=list(held)
        + [
            pltpu.VMEM((768, 256), BF16),
            pltpu.VMEM((256, 768), BF16),
            pltpu.VMEM((256, 768), BF16),
            pltpu.VMEM((256, 768), BF16),
            pltpu.VMEM((256, 512), BF16),
            pltpu.VMEM((256, 256), BF16),
            pltpu.VMEM((3, 256, 256), F32),
            pltpu.VMEM((3, 256, 256), F32),
            pltpu.VMEM((3, 256, 256), F32),
            pltpu.VMEM((STAGES[0][1], 128), F32),
            pltpu.VMEM((STAGES[1][1], 128), F32),
            pltpu.SemaphoreType.DMA((11,)),
            pltpu.SemaphoreType.DMA((3, 4)),
            pltpu.SemaphoreType.DMA((3, 4)),
            pltpu.SemaphoreType.DMA((2,)),
            pltpu.SemaphoreType.DMA((2,)),
        ],
        compiler_params=pltpu.CompilerParams(
            collective_id=0, has_side_effects=True, vmem_limit_bytes=48 * 1024 * 1024
        ),
        name="conjugate_gradient",
    )(*operands)


def solution(mesh):
    placed = (
        P("dom", None),
        P("dom", None),
        P("dom"),
        P(),
        P(),
        P("dom", None, None, None),
        P("dom", None),
        P("dom"),
        P("dom", None),
        P("dom", None, None),
        P("dom", None),
        P("dom", None, None, None),
    )
    return jax.shard_map(
        local, mesh=mesh, in_specs=placed, out_specs=P("dom", None), check_vma=False
    )
```

```python
import functools

import jax
import jax.numpy as jnp
from jax import lax
from jax.experimental import pallas as pl
from jax.experimental.pallas import tpu as pltpu
from jax.sharding import PartitionSpec as P

MESH = pl.DeviceIdType.MESH
GRID_W = 16
OFFSETS = (1, -1, GRID_W, -GRID_W)
REVERSE = (1, 0, 3, 2)
STAGES = ((1, 16), (16, 32))
F32 = jnp.float32
BF16 = jnp.bfloat16


def ring(distance, size):
    return min(distance, size - distance)


def farthest_first(stride, size):
    def hops(mask):
        if stride == 1:
            return max(ring(abs((a ^ mask) // 2 - a // 2), size // 2) for a in range(size))
        return max(
            ring(abs((a ^ mask) % 8 - a % 8), 8) + ring(abs((a ^ mask) // 8 - a // 8), size // 8)
            for a in range(size)
        )

    return sorted(range(1, size), key=lambda mask: -hops(mask))


def split(value):
    high = value.astype(BF16)
    low = (value - high.astype(F32)).astype(BF16)
    return high, low


def as_left(value):
    high, low = split(value)
    return jnp.concatenate([high, low, high], axis=1)


def as_right(value):
    high, low = split(value)
    return jnp.concatenate([high, low, high], axis=0)


def keep_left(ref, value):
    high, low = split(value)
    n = value.shape[1]
    ref[:, 0:n] = high
    ref[:, n : 2 * n] = high
    ref[:, 2 * n : 3 * n] = low


def keep_right(ref, value):
    high, low = split(value)
    n = value.shape[0]
    ref[0:n, :] = high
    ref[n : 2 * n, :] = high
    ref[2 * n : 3 * n, :] = low


def dot(a, b):
    return jnp.dot(a, b, preferred_element_type=F32)


def fold(value):
    rows, lanes = value.shape
    tile = jnp.sum(value.reshape(rows // 8, 8, lanes), axis=0)
    tile = tile[:, 0:128] + tile[:, 128:256]
    return jnp.sum(tile, axis=0, keepdims=True)


def total_of(row):
    return jnp.sum(row, axis=1, keepdims=True)


def kernel(
    right_hbm,
    noise_hbm,
    degree_hbm,
    dependence_ref,
    var_hbm,
    tiles_hbm,
    cols_hbm,
    count_hbm,
    border_hbm,
    rows_hbm,
    live_hbm,
    halo_hbm,
    out_ref,
    right_ref,
    noise_ref,
    degree_ref,
    var_ref,
    tiles_ref,
    cols_ref,
    count_ref,
    border_ref,
    rows_ref,
    live_ref,
    halo_ref,
    var_cat,
    local_cat,
    halo_cat,
    hop_cat,
    scatter,
    gather,
    basis,
    sent,
    received,
    sums_a,
    sums_b,
    load_sem,
    send_sem,
    recv_sem,
    sum_send_sem,
    sum_recv_sem,
):
    me = lax.axis_index("dom")
    pairs = {
        "right": (right_hbm, right_ref),
        "noise": (noise_hbm, noise_ref),
        "degree": (degree_hbm, degree_ref),
        "var": (var_hbm, var_ref),
        "tiles": (tiles_hbm, tiles_ref),
        "cols": (cols_hbm, cols_ref),
        "count": (count_hbm, count_ref),
        "border": (border_hbm, border_ref),
        "rows": (rows_hbm, rows_ref),
        "live": (live_hbm, live_ref),
        "halo": (halo_hbm, halo_ref),
    }
    loads = {
        name: pltpu.make_async_copy(src, dst, load_sem.at[i])
        for i, (name, (src, dst)) in enumerate(pairs.items())
    }
    for name in ("border", "halo", "right"):
        loads[name].start()

    column = jnp.bitwise_and(me, GRID_W - 1)
    line = jnp.right_shift(me, 4)
    usable = (column < GRID_W - 1, column > 0, line < 512 // GRID_W - 1, line > 0)

    odd = jnp.bitwise_and(me, 1)

    def partners(stride, size):
        return [(j, jnp.bitwise_xor(me, j * stride)) for j in farthest_first(stride, size)]

    barrier = pltpu.get_barrier_semaphore()
    for c in range(4):

        @pl.when(usable[c])
        def _():
            pl.semaphore_signal(barrier, inc=1, device_id=(me + OFFSETS[c],), device_id_type=MESH)

    greeted = 0
    for stride, size in STAGES:
        for _, partner in partners(stride, size):
            pl.semaphore_signal(barrier, inc=1, device_id=(partner,), device_id_type=MESH)
            greeted += 1

    for name in ("var", "live", "rows", "tiles", "cols", "count", "degree", "noise"):
        loads[name].start()

    for c in range(4):

        @pl.when(jnp.logical_not(usable[c]))
        def _():
            for k in range(2):
                received[k, 64 * c : 64 * c + 64, :] = jnp.zeros((64, 256), F32)

    loads["border"].wait()
    loads["halo"].wait()
    for c in range(4):
        tile = border_ref[0, c]
        weights = halo_ref[0, c]
        block = jnp.concatenate(
            [jnp.where(tile == r, weights, jnp.zeros_like(weights)) for r in range(2)], axis=1
        )
        keep_left(halo_cat.at[64 * c : 64 * c + 64, :], block)
    loads["right"].wait()
    field = right_ref[...]
    field_cat = as_right(field)
    outgoing = dot(halo_cat[...], field_cat)

    pl.semaphore_wait(barrier, greeted + sum(u.astype(jnp.int32) for u in usable))

    def copy(k, c, to):
        return pltpu.make_async_remote_copy(
            src_ref=sent.at[k, 64 * c : 64 * c + 64, :],
            dst_ref=received.at[k, 64 * to : 64 * to + 64, :],
            send_sem=send_sem.at[k, c],
            recv_sem=recv_sem.at[k, to],
            device_id=(me + OFFSETS[c],),
            device_id_type=MESH,
        )

    groups = ((0, 1), (2, 3))

    def start(k, group):
        for c in groups[group]:
            pl.when(usable[c])(copy(k, c, REVERSE[c]).start)

    def finish(k, group):
        for c in groups[group]:
            pl.when(usable[c])(copy(k, c, c).wait_recv)

    def last(i, device):
        i = 1 - i
        return pltpu.make_async_remote_copy(
            src_ref=sent.at[2, 64 * i : 64 * i + 64, :],
            dst_ref=received.at[2, 64 * i : 64 * i + 64, :],
            send_sem=send_sem.at[2, i],
            recv_sem=recv_sem.at[2, i],
            device_id=(device,),
            device_id_type=MESH,
        )

    across = GRID_W * (2 * odd - 1)
    down, up = usable[3], usable[2]
    even = odd == 0
    crosses = jnp.logical_or(jnp.logical_and(even, down), jnp.logical_and(odd == 1, up))
    crossed = jnp.logical_or(jnp.logical_and(even, up), jnp.logical_and(odd == 1, down))
    from_slots = pl.ds(pl.multiple_of(192 - 64 * odd, 64), 64)
    to_slots = pl.ds(pl.multiple_of(128 + 64 * odd, 64), 64)

    @pl.when(jnp.logical_not(usable[0]))
    def _():
        received[2, 64:128, :] = jnp.zeros((64, 256), F32)

    @pl.when(jnp.logical_not(crossed))
    def _():
        received[2, 0:64, :] = jnp.zeros((64, 256), F32)

    sent[0] = outgoing
    start(0, 1)
    start(0, 0)

    loads["var"].wait()
    keep_right(var_cat, var_ref[...])

    loads["live"].wait()
    loads["rows"].wait()
    places = []
    slot = lax.broadcasted_iota(jnp.int32, (1, 64), 1)
    for c in range(4):
        place = rows_ref[0, c : c + 1, :] + border_ref[0, c] * 128
        places.append(jnp.where(slot < live_ref[0, c], place, -1))
    places = jnp.concatenate(places, axis=1)
    hot = lax.broadcasted_iota(jnp.int32, (256, 256), 0) == places
    hot_wide = jnp.where(hot, 1.0, 0.0)
    hot = hot_wide.astype(BF16)
    for group in range(2):
        scatter[group, :, 0:128] = hot[:, 128 * group : 128 * group + 128]
        scatter[group, :, 128:256] = hot[:, 128 * group : 128 * group + 128]

    for name in ("tiles", "cols", "count", "degree"):
        loads[name].wait()
    dependence = dependence_ref[0]
    on_diagonal = lax.broadcasted_iota(jnp.int32, (256, 256), 0) == lax.broadcasted_iota(
        jnp.int32, (256, 256), 1
    )
    diagonal = jnp.where(on_diagonal, degree_ref[...], 0.0)
    for r in range(2):
        row = []
        for s in range(2):
            block = jnp.zeros((128, 128), F32)
            for j in range(2):
                used = jnp.logical_and(cols_ref[r, j] == s, count_ref[r] > j)
                block = jnp.where(used, tiles_ref[r, j], block)
            row.append(block)
        block_row = diagonal[128 * r : 128 * r + 128] - dependence * jnp.concatenate(row, axis=1)
        keep_left(local_cat.at[128 * r : 128 * r + 128, :], block_row)
    loads["noise"].wait()
    noise = noise_ref[...].astype(F32)

    hop_high = dot(halo_cat[:, 0:256], hot).astype(BF16)
    hop_low = dot(halo_cat[:, 512:768], hot).astype(BF16)
    for group in range(2):
        part = slice(128 * group, 128 * group + 128)
        hop_cat[group, :, 0:128] = hop_high[:, part]
        hop_cat[group, :, 128:256] = hop_high[:, part]
        hop_cat[group, :, 256:384] = hop_low[:, part]
    gather[...] = hot_wide.T.astype(BF16)

    basis[0] = field
    moments = [fold(field * field)]
    for k in range(2):
        near = dot(as_left(dot(local_cat[...], field_cat)), var_cat[...]) + noise * field
        next_near = dot(halo_cat[...], as_right(near))
        finish(k, 0)
        first = as_right(dot(as_left(received[k, 0:128, :]), var_cat[...]))
        image = near - dependence * dot(scatter[0], first[0:256])
        if k == 0:
            ready = next_near - dependence * dot(hop_cat[0], first)
        else:
            rows = jnp.concatenate([hop_cat[0, from_slots, :], hop_cat[0, 64:128, :]], axis=0)
            crossing = jnp.where(even, next_near[192:256], next_near[128:192])
            ready = jnp.concatenate([crossing, next_near[64:128]], axis=0)
            ready = ready - dependence * dot(rows, first)
        finish(k, 1)
        second = as_right(dot(as_left(received[k, 128:256, :]), var_cat[...]))
        if k == 0:
            for group in (1, 0):
                part = slice(128 * group, 128 * group + 128)
                sent[1, part, :] = ready[part] - dependence * dot(hop_cat[1, part, :], second)
                start(1, group)
        else:
            rows = jnp.concatenate([hop_cat[1, from_slots, :], hop_cat[1, 64:128, :]], axis=0)
            sent[2, 0:128, :] = ready - dependence * dot(rows, second)
            pl.when(crosses)(last(1, me + across).start)
            pl.when(usable[1])(last(0, me - 1).start)
        image = image - dependence * dot(scatter[1], second[0:256])
        moments.append(fold(field * image))
        moments.append(fold(image * image))
        field = image
        field_cat = as_right(field)
        basis[k + 1] = field

    mapped = dot(as_left(field), var_cat[...])
    near = fold(dot(local_cat[...], field_cat) * mapped + noise * (field * field))
    high, low = split(mapped)
    picks = jnp.concatenate([gather[to_slots, :], gather[0:64, :]], axis=0)
    picked = dot(picks, high) + dot(picks, low)
    picked = (-2.0 * dependence) * picked
    lane = lax.broadcasted_iota(jnp.int32, (8, 128), 1)
    line_of = lax.broadcasted_iota(jnp.int32, (8, 128), 0)

    def pack(rows):
        tile = jnp.sum(jnp.concatenate(rows, axis=0), axis=1, keepdims=True)
        return jnp.sum(jnp.where(lane == line_of, tile, 0.0), axis=0, keepdims=True)

    early = pack(moments + [near, jnp.zeros((2, 128), F32)])
    pl.when(usable[0])(last(0, me + 1).wait_recv)
    pl.when(crossed)(last(1, me - across).wait_recv)
    cross = fold(picked * received[2, 0:128, :])
    total = early + jnp.where(lane[0:1] == 5, total_of(cross), 0.0)

    pending = []
    for n, ((stride, size), sums) in enumerate(zip(STAGES, (sums_a, sums_b))):
        sums[0:1, :] = total
        for j, partner in partners(stride, size):
            pltpu.make_async_remote_copy(
                src_ref=sums.at[0:1, :],
                dst_ref=sums.at[j : j + 1, :],
                send_sem=sum_send_sem.at[n],
                recv_sem=sum_recv_sem.at[n],
                device_id=(partner,),
                device_id_type=MESH,
            ).start()
        whole = pltpu.make_async_remote_copy(
            src_ref=sums.at[1:size, :],
            dst_ref=sums.at[1:size, :],
            send_sem=sum_send_sem.at[n],
            recv_sem=sum_recv_sem.at[n],
            device_id=(me,),
            device_id_type=MESH,
        )
        whole.wait_recv()
        total = jnp.sum(sums[...], axis=0, keepdims=True)
        pending.append(whole)

    m = [total[:, k : k + 1] for k in range(6)]
    a0 = m[0] / m[1]
    rr1 = m[0] - 2.0 * a0 * m[1] + a0 * a0 * m[2]
    g0 = 1.0 + rr1 / m[0]
    g1 = -a0
    a1 = rr1 / (g0 * g0 * m[1] + 2.0 * g0 * g1 * m[2] + g1 * g1 * m[3])
    e1 = -a0 - a1 * g0
    e2 = -a1 * g1
    rr2 = (
        m[0] + 2.0 * e1 * m[1] + (e1 * e1 + 2.0 * e2) * m[2] + 2.0 * e1 * e2 * m[3] + e2 * e2 * m[4]
    )
    b1 = rr2 / rr1
    f0 = 1.0 + b1 * g0
    f1 = e1 + b1 * g1
    f2 = e2
    a2 = rr2 / (
        f0 * f0 * m[1]
        + 2.0 * f0 * f1 * m[2]
        + (f1 * f1 + 2.0 * f0 * f2) * m[3]
        + 2.0 * f1 * f2 * m[4]
        + f2 * f2 * m[5]
    )
    c0 = a0 + a1 * g0 + a2 * f0
    c1 = a1 * g1 + a2 * f1
    c2 = a2 * f2
    out_ref[...] = c0 * basis[0] + c1 * basis[1] + c2 * basis[2]

    for whole in pending:
        whole.wait_send()
    for k in range(2):
        for c in range(4):
            pl.when(usable[c])(copy(k, c, REVERSE[c]).wait_send)
    pl.when(usable[1])(last(0, me - 1).wait_send)
    pl.when(crosses)(last(1, me + across).wait_send)


def local(
    right_side,
    noise_precision,
    degree,
    dependence,
    var_precision,
    local_tiles,
    tile_cols,
    tile_count,
    halo_tile,
    send_rows,
    send_count,
    halo_weights,
):
    operands = (
        right_side,
        noise_precision,
        degree.reshape(1, 256),
        dependence.reshape(1),
        var_precision,
        local_tiles,
        tile_cols,
        tile_count,
        halo_tile,
        send_rows,
        send_count,
        halo_weights,
    )
    operands = [
        x if x.size == 1 else pltpu.with_memory_space_constraint(x, pltpu.HBM) for x in operands
    ]
    specs = [pl.BlockSpec(memory_space=pltpu.SMEM if x.size == 1 else pltpu.HBM) for x in operands]
    held = (
        pltpu.VMEM((256, 256), F32),
        pltpu.VMEM((256, 256), BF16),
        pltpu.VMEM((1, 256), F32),
        pltpu.VMEM((256, 256), F32),
        pltpu.VMEM((2, 2, 128, 128), F32),
        pltpu.SMEM((2, 2), jnp.int32),
        pltpu.SMEM((2,), jnp.int32),
        pltpu.SMEM((1, 4), jnp.int32),
        pltpu.VMEM((1, 4, 64), jnp.int32),
        pltpu.SMEM((1, 4), jnp.int32),
        pltpu.VMEM((1, 4, 64, 128), F32),
    )
    return pl.pallas_call(
        kernel,
        out_shape=pltpu.VMEM((256, 256), F32),
        in_specs=specs,
        out_specs=pl.BlockSpec(memory_space=pltpu.VMEM),
        scratch_shapes=list(held)
        + [
            pltpu.VMEM((768, 256), BF16),
            pltpu.VMEM((256, 768), BF16),
            pltpu.VMEM((256, 768), BF16),
            pltpu.VMEM((2, 256, 384), BF16),
            pltpu.VMEM((2, 256, 256), BF16),
            pltpu.VMEM((256, 256), BF16),
            pltpu.VMEM((3, 256, 256), F32),
            pltpu.VMEM((3, 256, 256), F32),
            pltpu.VMEM((3, 256, 256), F32),
            pltpu.VMEM((STAGES[0][1], 128), F32),
            pltpu.VMEM((STAGES[1][1], 128), F32),
            pltpu.SemaphoreType.DMA((11,)),
            pltpu.SemaphoreType.DMA((3, 4)),
            pltpu.SemaphoreType.DMA((3, 4)),
            pltpu.SemaphoreType.DMA((2,)),
            pltpu.SemaphoreType.DMA((2,)),
        ],
        compiler_params=pltpu.CompilerParams(
            collective_id=0, has_side_effects=True, vmem_limit_bytes=48 * 1024 * 1024
        ),
        name="conjugate_gradient",
    )(*operands)


def solution(mesh):
    placed = (
        P("dom", None),
        P("dom", None),
        P("dom"),
        P(),
        P(),
        P("dom", None, None, None),
        P("dom", None),
        P("dom"),
        P("dom", None),
        P("dom", None, None),
        P("dom", None),
        P("dom", None, None, None),
    )
    return jax.shard_map(
        local, mesh=mesh, in_specs=placed, out_specs=P("dom", None), check_vma=False
    )
```

```python
import functools

import jax
import jax.numpy as jnp
from jax import lax
from jax.experimental import pallas as pl
from jax.experimental.pallas import tpu as pltpu
from jax.sharding import PartitionSpec as P

MESH = pl.DeviceIdType.MESH
GRID_W = 16
OFFSETS = (1, -1, GRID_W, -GRID_W)
REVERSE = (1, 0, 3, 2)
STAGES = ((1, 16), (16, 32))
F32 = jnp.float32
BF16 = jnp.bfloat16


def partners_by_bit():
    groups = {}
    for mask in range(1, 16):
        groups.setdefault(1 << (mask.bit_length() - 1), []).append(mask)
    for z in range(8):
        for x in range(4):
            if z or x:
                bit = 16 << (z.bit_length() - 1) if z else 128 << (x.bit_length() - 1)
                groups.setdefault(bit, []).append(16 * z + 128 * x)
    return groups


def ring(distance, size):
    return min(distance, size - distance)


def farthest_first(stride, size):
    def hops(mask):
        if stride == 1:
            return max(ring(abs((a ^ mask) // 2 - a // 2), size // 2) for a in range(size))
        return max(
            ring(abs((a ^ mask) % 8 - a % 8), 8) + ring(abs((a ^ mask) // 8 - a // 8), size // 8)
            for a in range(size)
        )

    return sorted(range(1, size), key=lambda mask: -hops(mask))


def split(value):
    high = value.astype(BF16)
    low = (value - high.astype(F32)).astype(BF16)
    return high, low


def as_left(value):
    high, low = split(value)
    return jnp.concatenate([high, low, high], axis=1)


def as_right(value):
    high, low = split(value)
    return jnp.concatenate([high, low, high], axis=0)


def keep_left(ref, value):
    high, low = split(value)
    n = value.shape[1]
    ref[:, 0:n] = high
    ref[:, n : 2 * n] = high
    ref[:, 2 * n : 3 * n] = low


def keep_right(ref, value):
    high, low = split(value)
    n = value.shape[0]
    ref[0:n, :] = high
    ref[n : 2 * n, :] = high
    ref[2 * n : 3 * n, :] = low


def dot(a, b):
    return jnp.dot(a, b, preferred_element_type=F32)


def fold(value):
    rows, lanes = value.shape
    tile = jnp.sum(value.reshape(rows // 8, 8, lanes), axis=0)
    tile = tile[:, 0:128] + tile[:, 128:256]
    return jnp.sum(tile, axis=0, keepdims=True)


def total_of(row):
    return jnp.sum(row, axis=1, keepdims=True)


def kernel(
    right_hbm,
    noise_hbm,
    degree_hbm,
    dependence_ref,
    var_hbm,
    tiles_hbm,
    cols_hbm,
    count_hbm,
    border_hbm,
    rows_hbm,
    live_hbm,
    halo_hbm,
    out_ref,
    right_ref,
    noise_ref,
    degree_ref,
    var_ref,
    tiles_ref,
    cols_ref,
    count_ref,
    border_ref,
    rows_ref,
    live_ref,
    halo_ref,
    var_cat,
    local_cat,
    halo_cat,
    hop_cat,
    scatter,
    gather,
    basis,
    sent,
    received,
    sums_a,
    sums_b,
    load_sem,
    send_sem,
    recv_sem,
    sum_send_sem,
    sum_recv_sem,
    answer_sem,
):
    me = lax.axis_index("dom")
    pairs = {
        "right": (right_hbm, right_ref),
        "noise": (noise_hbm, noise_ref),
        "degree": (degree_hbm, degree_ref),
        "var": (var_hbm, var_ref),
        "tiles": (tiles_hbm, tiles_ref),
        "cols": (cols_hbm, cols_ref),
        "count": (count_hbm, count_ref),
        "border": (border_hbm, border_ref),
        "rows": (rows_hbm, rows_ref),
        "live": (live_hbm, live_ref),
        "halo": (halo_hbm, halo_ref),
    }
    loads = {
        name: pltpu.make_async_copy(src, dst, load_sem.at[i])
        for i, (name, (src, dst)) in enumerate(pairs.items())
    }
    for name in ("border", "halo", "right"):
        loads[name].start()

    column = jnp.bitwise_and(me, GRID_W - 1)
    line = jnp.right_shift(me, 4)
    usable = (column < GRID_W - 1, column > 0, line < 512 // GRID_W - 1, line > 0)

    odd = jnp.bitwise_and(me, 1)

    def partners(stride, size):
        return [(j, jnp.bitwise_xor(me, j * stride)) for j in farthest_first(stride, size)]

    barrier = pltpu.get_barrier_semaphore()
    for c in range(4):

        @pl.when(usable[c])
        def _():
            pl.semaphore_signal(barrier, inc=1, device_id=(me + OFFSETS[c],), device_id_type=MESH)

    for bit, masks in partners_by_bit().items():

        @pl.when(jnp.bitwise_and(me, bit) == 0)
        def _():
            for mask in masks:
                greet = jnp.bitwise_xor(me, mask)
                pl.semaphore_signal(barrier, inc=1, device_id=(greet,), device_id_type=MESH)

    earlier = column + 4 * jnp.bitwise_and(line, 7) + jnp.right_shift(me, 7)

    for name in ("var", "live", "rows", "tiles", "cols", "count", "degree", "noise"):
        loads[name].start()

    for c in range(4):

        @pl.when(jnp.logical_not(usable[c]))
        def _():
            for k in range(2):
                received[k, 64 * c : 64 * c + 64, :] = jnp.zeros((64, 256), F32)

    loads["border"].wait()
    loads["halo"].wait()
    for c in range(4):
        tile = border_ref[0, c]
        weights = halo_ref[0, c]
        block = jnp.concatenate(
            [jnp.where(tile == r, weights, jnp.zeros_like(weights)) for r in range(2)], axis=1
        )
        keep_left(halo_cat.at[64 * c : 64 * c + 64, :], block)
    loads["right"].wait()
    field = right_ref[...]
    field_cat = as_right(field)
    outgoing = dot(halo_cat[...], field_cat)

    pl.semaphore_wait(barrier, earlier + sum(u.astype(jnp.int32) for u in usable))

    def copy(k, c, to):
        return pltpu.make_async_remote_copy(
            src_ref=sent.at[k, 64 * c : 64 * c + 64, :],
            dst_ref=received.at[k, 64 * to : 64 * to + 64, :],
            send_sem=send_sem.at[k, c],
            recv_sem=recv_sem.at[k, to],
            device_id=(me + OFFSETS[c],),
            device_id_type=MESH,
        )

    groups = ((0, 1), (2, 3))

    def start(k, group):
        for c in groups[group]:
            pl.when(usable[c])(copy(k, c, REVERSE[c]).start)

    def finish(k, group):
        for c in groups[group]:
            pl.when(usable[c])(copy(k, c, c).wait_recv)

    def last(i, device):
        i = 1 - i
        return pltpu.make_async_remote_copy(
            src_ref=sent.at[2, 64 * i : 64 * i + 64, :],
            dst_ref=received.at[2, 64 * i : 64 * i + 64, :],
            send_sem=send_sem.at[2, i],
            recv_sem=recv_sem.at[2, i],
            device_id=(device,),
            device_id_type=MESH,
        )

    across = GRID_W * (2 * odd - 1)
    down, up = usable[3], usable[2]
    even = odd == 0
    crosses = jnp.logical_or(jnp.logical_and(even, down), jnp.logical_and(odd == 1, up))
    crossed = jnp.logical_or(jnp.logical_and(even, up), jnp.logical_and(odd == 1, down))
    from_slots = pl.ds(pl.multiple_of(192 - 64 * odd, 64), 64)
    to_slots = pl.ds(pl.multiple_of(128 + 64 * odd, 64), 64)

    @pl.when(jnp.logical_not(usable[0]))
    def _():
        received[2, 64:128, :] = jnp.zeros((64, 256), F32)

    @pl.when(jnp.logical_not(crossed))
    def _():
        received[2, 0:64, :] = jnp.zeros((64, 256), F32)

    sent[0] = outgoing
    start(0, 1)
    start(0, 0)

    for bit, masks in partners_by_bit().items():

        @pl.when(jnp.bitwise_and(me, bit) != 0)
        def _():
            for mask in masks:
                answer = jnp.bitwise_xor(me, mask)
                pl.semaphore_signal(answer_sem, inc=1, device_id=(answer,), device_id_type=MESH)


    loads["var"].wait()
    keep_right(var_cat, var_ref[...])

    loads["live"].wait()
    loads["rows"].wait()
    places = []
    slot = lax.broadcasted_iota(jnp.int32, (1, 64), 1)
    for c in range(4):
        place = rows_ref[0, c : c + 1, :] + border_ref[0, c] * 128
        places.append(jnp.where(slot < live_ref[0, c], place, -1))
    places = jnp.concatenate(places, axis=1)
    hot = lax.broadcasted_iota(jnp.int32, (256, 256), 0) == places
    hot_wide = jnp.where(hot, 1.0, 0.0)
    hot = hot_wide.astype(BF16)
    for group in range(2):
        scatter[group, :, 0:128] = hot[:, 128 * group : 128 * group + 128]
        scatter[group, :, 128:256] = hot[:, 128 * group : 128 * group + 128]

    for name in ("tiles", "cols", "count", "degree"):
        loads[name].wait()
    dependence = dependence_ref[0]
    on_diagonal = lax.broadcasted_iota(jnp.int32, (256, 256), 0) == lax.broadcasted_iota(
        jnp.int32, (256, 256), 1
    )
    diagonal = jnp.where(on_diagonal, degree_ref[...], 0.0)
    for r in range(2):
        row = []
        for s in range(2):
            block = jnp.zeros((128, 128), F32)
            for j in range(2):
                used = jnp.logical_and(cols_ref[r, j] == s, count_ref[r] > j)
                block = jnp.where(used, tiles_ref[r, j], block)
            row.append(block)
        block_row = diagonal[128 * r : 128 * r + 128] - dependence * jnp.concatenate(row, axis=1)
        keep_left(local_cat.at[128 * r : 128 * r + 128, :], block_row)
    loads["noise"].wait()
    noise = noise_ref[...].astype(F32)

    hop_high = dot(halo_cat[:, 0:256], hot).astype(BF16)
    hop_low = dot(halo_cat[:, 512:768], hot).astype(BF16)
    for group in range(2):
        part = slice(128 * group, 128 * group + 128)
        hop_cat[group, :, 0:128] = hop_high[:, part]
        hop_cat[group, :, 128:256] = hop_high[:, part]
        hop_cat[group, :, 256:384] = hop_low[:, part]
    gather[...] = hot_wide.T.astype(BF16)

    basis[0] = field
    moments = [fold(field * field)]
    for k in range(2):
        near = dot(as_left(dot(local_cat[...], field_cat)), var_cat[...]) + noise * field
        next_near = dot(halo_cat[...], as_right(near))
        finish(k, 0)
        first = as_right(dot(as_left(received[k, 0:128, :]), var_cat[...]))
        image = near - dependence * dot(scatter[0], first[0:256])
        if k == 0:
            ready = next_near - dependence * dot(hop_cat[0], first)
        else:
            rows = jnp.concatenate([hop_cat[0, from_slots, :], hop_cat[0, 64:128, :]], axis=0)
            crossing = jnp.where(even, next_near[192:256], next_near[128:192])
            ready = jnp.concatenate([crossing, next_near[64:128]], axis=0)
            ready = ready - dependence * dot(rows, first)
        finish(k, 1)
        second = as_right(dot(as_left(received[k, 128:256, :]), var_cat[...]))
        if k == 0:
            for group in (1, 0):
                part = slice(128 * group, 128 * group + 128)
                sent[1, part, :] = ready[part] - dependence * dot(hop_cat[1, part, :], second)
                start(1, group)
        else:
            rows = jnp.concatenate([hop_cat[1, from_slots, :], hop_cat[1, 64:128, :]], axis=0)
            sent[2, 0:128, :] = ready - dependence * dot(rows, second)
            pl.when(crosses)(last(1, me + across).start)
            pl.when(usable[1])(last(0, me - 1).start)
        image = image - dependence * dot(scatter[1], second[0:256])
        moments.append(fold(field * image))
        moments.append(fold(image * image))
        field = image
        field_cat = as_right(field)
        basis[k + 1] = field

    mapped = dot(as_left(field), var_cat[...])
    near = fold(dot(local_cat[...], field_cat) * mapped + noise * (field * field))
    high, low = split(mapped)
    picks = jnp.concatenate([gather[to_slots, :], gather[0:64, :]], axis=0)
    picked = dot(picks, high) + dot(picks, low)
    picked = (-2.0 * dependence) * picked
    lane = lax.broadcasted_iota(jnp.int32, (8, 128), 1)
    line_of = lax.broadcasted_iota(jnp.int32, (8, 128), 0)

    def pack(rows):
        tile = jnp.sum(jnp.concatenate(rows, axis=0), axis=1, keepdims=True)
        return jnp.sum(jnp.where(lane == line_of, tile, 0.0), axis=0, keepdims=True)

    early = pack(moments + [near, jnp.zeros((2, 128), F32)])
    pl.when(usable[0])(last(0, me + 1).wait_recv)
    pl.when(crossed)(last(1, me - across).wait_recv)
    cross = fold(picked * received[2, 0:128, :])
    later = sum(size - 1 for _, size in STAGES) - earlier

    @pl.when(later > 0)
    def _():
        pl.semaphore_wait(answer_sem, later)

    total = early + jnp.where(lane[0:1] == 5, total_of(cross), 0.0)

    pending = []
    for n, ((stride, size), sums) in enumerate(zip(STAGES, (sums_a, sums_b))):
        sums[0:1, :] = total
        for j, partner in partners(stride, size):
            pltpu.make_async_remote_copy(
                src_ref=sums.at[0:1, :],
                dst_ref=sums.at[j : j + 1, :],
                send_sem=sum_send_sem.at[n],
                recv_sem=sum_recv_sem.at[n],
                device_id=(partner,),
                device_id_type=MESH,
            ).start()
        whole = pltpu.make_async_remote_copy(
            src_ref=sums.at[1:size, :],
            dst_ref=sums.at[1:size, :],
            send_sem=sum_send_sem.at[n],
            recv_sem=sum_recv_sem.at[n],
            device_id=(me,),
            device_id_type=MESH,
        )
        whole.wait_recv()
        total = jnp.sum(sums[...], axis=0, keepdims=True)
        pending.append(whole)

    m = [total[:, k : k + 1] for k in range(6)]
    a0 = m[0] / m[1]
    rr1 = m[0] - 2.0 * a0 * m[1] + a0 * a0 * m[2]
    g0 = 1.0 + rr1 / m[0]
    g1 = -a0
    a1 = rr1 / (g0 * g0 * m[1] + 2.0 * g0 * g1 * m[2] + g1 * g1 * m[3])
    e1 = -a0 - a1 * g0
    e2 = -a1 * g1
    rr2 = (
        m[0] + 2.0 * e1 * m[1] + (e1 * e1 + 2.0 * e2) * m[2] + 2.0 * e1 * e2 * m[3] + e2 * e2 * m[4]
    )
    b1 = rr2 / rr1
    f0 = 1.0 + b1 * g0
    f1 = e1 + b1 * g1
    f2 = e2
    a2 = rr2 / (
        f0 * f0 * m[1]
        + 2.0 * f0 * f1 * m[2]
        + (f1 * f1 + 2.0 * f0 * f2) * m[3]
        + 2.0 * f1 * f2 * m[4]
        + f2 * f2 * m[5]
    )
    c0 = a0 + a1 * g0 + a2 * f0
    c1 = a1 * g1 + a2 * f1
    c2 = a2 * f2
    out_ref[...] = c0 * basis[0] + c1 * basis[1] + c2 * basis[2]

    for whole in pending:
        whole.wait_send()
    for k in range(2):
        for c in range(4):
            pl.when(usable[c])(copy(k, c, REVERSE[c]).wait_send)
    pl.when(usable[1])(last(0, me - 1).wait_send)
    pl.when(crosses)(last(1, me + across).wait_send)


def local(
    right_side,
    noise_precision,
    degree,
    dependence,
    var_precision,
    local_tiles,
    tile_cols,
    tile_count,
    halo_tile,
    send_rows,
    send_count,
    halo_weights,
):
    operands = (
        right_side,
        noise_precision,
        degree.reshape(1, 256),
        dependence.reshape(1),
        var_precision,
        local_tiles,
        tile_cols,
        tile_count,
        halo_tile,
        send_rows,
        send_count,
        halo_weights,
    )
    operands = [
        x if x.size == 1 else pltpu.with_memory_space_constraint(x, pltpu.HBM) for x in operands
    ]
    specs = [pl.BlockSpec(memory_space=pltpu.SMEM if x.size == 1 else pltpu.HBM) for x in operands]
    held = (
        pltpu.VMEM((256, 256), F32),
        pltpu.VMEM((256, 256), BF16),
        pltpu.VMEM((1, 256), F32),
        pltpu.VMEM((256, 256), F32),
        pltpu.VMEM((2, 2, 128, 128), F32),
        pltpu.SMEM((2, 2), jnp.int32),
        pltpu.SMEM((2,), jnp.int32),
        pltpu.SMEM((1, 4), jnp.int32),
        pltpu.VMEM((1, 4, 64), jnp.int32),
        pltpu.SMEM((1, 4), jnp.int32),
        pltpu.VMEM((1, 4, 64, 128), F32),
    )
    return pl.pallas_call(
        kernel,
        out_shape=pltpu.VMEM((256, 256), F32),
        in_specs=specs,
        out_specs=pl.BlockSpec(memory_space=pltpu.VMEM),
        scratch_shapes=list(held)
        + [
            pltpu.VMEM((768, 256), BF16),
            pltpu.VMEM((256, 768), BF16),
            pltpu.VMEM((256, 768), BF16),
            pltpu.VMEM((2, 256, 384), BF16),
            pltpu.VMEM((2, 256, 256), BF16),
            pltpu.VMEM((256, 256), BF16),
            pltpu.VMEM((3, 256, 256), F32),
            pltpu.VMEM((3, 256, 256), F32),
            pltpu.VMEM((3, 256, 256), F32),
            pltpu.VMEM((STAGES[0][1], 128), F32),
            pltpu.VMEM((STAGES[1][1], 128), F32),
            pltpu.SemaphoreType.DMA((11,)),
            pltpu.SemaphoreType.DMA((3, 4)),
            pltpu.SemaphoreType.DMA((3, 4)),
            pltpu.SemaphoreType.DMA((2,)),
            pltpu.SemaphoreType.DMA((2,)),
            pltpu.SemaphoreType.REGULAR,
        ],
        compiler_params=pltpu.CompilerParams(
            collective_id=0, has_side_effects=True, vmem_limit_bytes=48 * 1024 * 1024
        ),
        name="conjugate_gradient",
    )(*operands)


def solution(mesh):
    placed = (
        P("dom", None),
        P("dom", None),
        P("dom"),
        P(),
        P(),
        P("dom", None, None, None),
        P("dom", None),
        P("dom"),
        P("dom", None),
        P("dom", None, None),
        P("dom", None),
        P("dom", None, None, None),
    )
    return jax.shard_map(
        local, mesh=mesh, in_specs=placed, out_specs=P("dom", None), check_vma=False
    )
```

```python
import functools

import jax
import jax.numpy as jnp
from jax import lax
from jax.experimental import pallas as pl
from jax.experimental.pallas import tpu as pltpu
from jax.sharding import PartitionSpec as P

MESH = pl.DeviceIdType.MESH
GRID_W = 16
OFFSETS = (1, -1, GRID_W, -GRID_W)
REVERSE = (1, 0, 3, 2)
STAGES = ((1, 16), (16, 32))
F32 = jnp.float32
BF16 = jnp.bfloat16


def partners_by_bit():
    groups = {}
    for mask in range(1, 16):
        groups.setdefault(1 << (mask.bit_length() - 1), []).append(mask)
    for z in range(8):
        for x in range(4):
            if z or x:
                bit = 16 << (z.bit_length() - 1) if z else 128 << (x.bit_length() - 1)
                groups.setdefault(bit, []).append(16 * z + 128 * x)
    return groups


def ring(distance, size):
    return min(distance, size - distance)


def farthest_first(stride, size):
    def hops(mask):
        if stride == 1:
            return max(ring(abs((a ^ mask) // 2 - a // 2), size // 2) for a in range(size))
        return max(
            ring(abs((a ^ mask) % 8 - a % 8), 8) + ring(abs((a ^ mask) // 8 - a // 8), size // 8)
            for a in range(size)
        )

    return sorted(range(1, size), key=lambda mask: -hops(mask))


def split(value):
    high = value.astype(BF16)
    low = (value - high.astype(F32)).astype(BF16)
    return high, low


def as_left(value):
    high, low = split(value)
    return jnp.concatenate([high, low, high], axis=1)


def as_right(value):
    high, low = split(value)
    return jnp.concatenate([high, low, high], axis=0)


def keep_left(ref, value):
    high, low = split(value)
    n = value.shape[1]
    ref[:, 0:n] = high
    ref[:, n : 2 * n] = high
    ref[:, 2 * n : 3 * n] = low


def keep_right(ref, value):
    high, low = split(value)
    n = value.shape[0]
    ref[0:n, :] = high
    ref[n : 2 * n, :] = high
    ref[2 * n : 3 * n, :] = low


def dot(a, b):
    return jnp.dot(a, b, preferred_element_type=F32)


def fold(value):
    rows, lanes = value.shape
    tile = jnp.sum(value.reshape(rows // 8, 8, lanes), axis=0)
    tile = tile[:, 0:128] + tile[:, 128:256]
    return jnp.sum(tile, axis=0, keepdims=True)


def total_of(row):
    return jnp.sum(row, axis=1, keepdims=True)


def kernel(
    right_hbm,
    noise_hbm,
    degree_hbm,
    dependence_ref,
    var_hbm,
    tiles_hbm,
    cols_hbm,
    count_hbm,
    border_hbm,
    rows_hbm,
    live_hbm,
    halo_hbm,
    out_ref,
    right_ref,
    noise_ref,
    degree_ref,
    var_ref,
    tiles_ref,
    cols_ref,
    count_ref,
    border_ref,
    rows_ref,
    live_ref,
    halo_ref,
    var_cat,
    local_cat,
    halo_cat,
    hop_cat,
    scatter,
    gather,
    basis,
    sent,
    received,
    sums_a,
    sums_b,
    load_sem,
    send_sem,
    recv_sem,
    sum_send_sem,
    sum_recv_sem,
    answer_sem,
):
    me = lax.axis_index("dom")
    pairs = {
        "right": (right_hbm.at[0:128, :], right_ref.at[0:128, :]),
        "right_too": (right_hbm.at[128:256, :], right_ref.at[128:256, :]),
        "noise": (noise_hbm, noise_ref),
        "degree": (degree_hbm, degree_ref),
        "var": (var_hbm, var_ref),
        "tiles": (tiles_hbm, tiles_ref),
        "cols": (cols_hbm, cols_ref),
        "count": (count_hbm, count_ref),
        "border": (border_hbm, border_ref),
        "rows": (rows_hbm, rows_ref),
        "live": (live_hbm, live_ref),
        "halo": (halo_hbm, halo_ref),
    }
    loads = {
        name: pltpu.make_async_copy(src, dst, load_sem.at[i])
        for i, (name, (src, dst)) in enumerate(pairs.items())
    }
    for name in ("right", "right_too", "halo", "border"):
        loads[name].start()

    column = jnp.bitwise_and(me, GRID_W - 1)
    line = jnp.right_shift(me, 4)
    usable = (column < GRID_W - 1, column > 0, line < 512 // GRID_W - 1, line > 0)

    odd = jnp.bitwise_and(me, 1)

    def partners(stride, size):
        return [(j, jnp.bitwise_xor(me, j * stride)) for j in farthest_first(stride, size)]

    barrier = pltpu.get_barrier_semaphore()
    for c in range(4):

        @pl.when(usable[c])
        def _():
            pl.semaphore_signal(barrier, inc=1, device_id=(me + OFFSETS[c],), device_id_type=MESH)

    for bit, masks in partners_by_bit().items():

        @pl.when(jnp.bitwise_and(me, bit) == 0)
        def _():
            for mask in masks:
                greet = jnp.bitwise_xor(me, mask)
                pl.semaphore_signal(barrier, inc=1, device_id=(greet,), device_id_type=MESH)

    earlier = column + 4 * jnp.bitwise_and(line, 7) + jnp.right_shift(me, 7)

    for name in ("var", "live", "rows", "tiles", "cols", "count", "degree", "noise"):
        loads[name].start()

    for c in range(4):

        @pl.when(jnp.logical_not(usable[c]))
        def _():
            for k in range(2):
                received[k, 64 * c : 64 * c + 64, :] = jnp.zeros((64, 256), F32)

    def copy(k, c, to):
        return pltpu.make_async_remote_copy(
            src_ref=sent.at[k, 64 * c : 64 * c + 64, :],
            dst_ref=received.at[k, 64 * to : 64 * to + 64, :],
            send_sem=send_sem.at[k, c],
            recv_sem=recv_sem.at[k, to],
            device_id=(me + OFFSETS[c],),
            device_id_type=MESH,
        )

    groups = ((0, 1), (2, 3))

    def start(k, group):
        for c in groups[group]:
            pl.when(usable[c])(copy(k, c, REVERSE[c]).start)

    def finish(k, group):
        for c in groups[group]:
            pl.when(usable[c])(copy(k, c, c).wait_recv)

    def last(i, device):
        i = 1 - i
        return pltpu.make_async_remote_copy(
            src_ref=sent.at[2, 64 * i : 64 * i + 64, :],
            dst_ref=received.at[2, 64 * i : 64 * i + 64, :],
            send_sem=send_sem.at[2, i],
            recv_sem=recv_sem.at[2, i],
            device_id=(device,),
            device_id_type=MESH,
        )

    across = GRID_W * (1 - 2 * odd)
    down, up = usable[3], usable[2]
    even = odd == 0
    crosses = jnp.logical_or(jnp.logical_and(even, up), jnp.logical_and(odd == 1, down))
    crossed = jnp.logical_or(jnp.logical_and(even, down), jnp.logical_and(odd == 1, up))
    from_slots = pl.ds(pl.multiple_of(128 + 64 * odd, 64), 64)
    to_slots = pl.ds(pl.multiple_of(192 - 64 * odd, 64), 64)

    @pl.when(jnp.logical_not(usable[1]))
    def _():
        received[2, 64:128, :] = jnp.zeros((64, 256), F32)

    @pl.when(jnp.logical_not(crossed))
    def _():
        received[2, 0:64, :] = jnp.zeros((64, 256), F32)

    loads["border"].wait()
    loads["halo"].wait()
    loads["right"].wait()
    loads["right_too"].wait()
    field = right_ref[...]
    field_cat = as_right(field)
    for group in (1, 0):
        for c in groups[group]:
            tile = border_ref[0, c]
            weights = halo_ref[0, c]
            block = jnp.concatenate(
                [jnp.where(tile == r, weights, jnp.zeros_like(weights)) for r in range(2)], axis=1
            )
            keep_left(halo_cat.at[64 * c : 64 * c + 64, :], block)
        part = slice(128 * group, 128 * group + 128)
        sent[0, part, :] = dot(halo_cat[part, :], field_cat)
        if group:
            pl.semaphore_wait(barrier, earlier + sum(u.astype(jnp.int32) for u in usable))
        start(0, group)

    for bit, masks in partners_by_bit().items():

        @pl.when(jnp.bitwise_and(me, bit) != 0)
        def _():
            for mask in masks:
                answer = jnp.bitwise_xor(me, mask)
                pl.semaphore_signal(answer_sem, inc=1, device_id=(answer,), device_id_type=MESH)


    loads["var"].wait()
    keep_right(var_cat, var_ref[...])

    loads["live"].wait()
    loads["rows"].wait()
    places = []
    slot = lax.broadcasted_iota(jnp.int32, (1, 64), 1)
    for c in range(4):
        place = rows_ref[0, c : c + 1, :] + border_ref[0, c] * 128
        places.append(jnp.where(slot < live_ref[0, c], place, -1))
    places = jnp.concatenate(places, axis=1)
    hot = lax.broadcasted_iota(jnp.int32, (256, 256), 0) == places
    hot_wide = jnp.where(hot, 1.0, 0.0)
    hot = hot_wide.astype(BF16)
    for group in range(2):
        scatter[group, :, 0:128] = hot[:, 128 * group : 128 * group + 128]
        scatter[group, :, 128:256] = hot[:, 128 * group : 128 * group + 128]

    for name in ("tiles", "cols", "count", "degree"):
        loads[name].wait()
    dependence = dependence_ref[0]
    on_diagonal = lax.broadcasted_iota(jnp.int32, (256, 256), 0) == lax.broadcasted_iota(
        jnp.int32, (256, 256), 1
    )
    diagonal = jnp.where(on_diagonal, degree_ref[...], 0.0)
    for r in range(2):
        row = []
        for s in range(2):
            block = jnp.zeros((128, 128), F32)
            for j in range(2):
                used = jnp.logical_and(cols_ref[r, j] == s, count_ref[r] > j)
                block = jnp.where(used, tiles_ref[r, j], block)
            row.append(block)
        block_row = diagonal[128 * r : 128 * r + 128] - dependence * jnp.concatenate(row, axis=1)
        keep_left(local_cat.at[128 * r : 128 * r + 128, :], block_row)
    loads["noise"].wait()
    noise = noise_ref[...].astype(F32)

    hop_high = dot(halo_cat[:, 0:256], hot).astype(BF16)
    hop_low = dot(halo_cat[:, 512:768], hot).astype(BF16)
    for group in range(2):
        part = slice(128 * group, 128 * group + 128)
        hop_cat[group, :, 0:128] = hop_high[:, part]
        hop_cat[group, :, 128:256] = hop_high[:, part]
        hop_cat[group, :, 256:384] = hop_low[:, part]
    gather[...] = hot_wide.T.astype(BF16)

    basis[0] = field
    moments = [fold(field * field)]
    for k in range(2):
        near = dot(as_left(dot(local_cat[...], field_cat)), var_cat[...]) + noise * field
        next_near = dot(halo_cat[...], as_right(near))
        finish(k, 0)
        first = as_right(dot(as_left(received[k, 0:128, :]), var_cat[...]))
        image = near - dependence * dot(scatter[0], first[0:256])
        if k == 0:
            ready = next_near - dependence * dot(hop_cat[0], first)
        else:
            rows = jnp.concatenate([hop_cat[0, from_slots, :], hop_cat[0, 0:64, :]], axis=0)
            crossing = jnp.where(even, next_near[128:192], next_near[192:256])
            ready = jnp.concatenate([crossing, next_near[0:64]], axis=0)
            ready = ready - dependence * dot(rows, first)
        finish(k, 1)
        second = as_right(dot(as_left(received[k, 128:256, :]), var_cat[...]))
        if k == 0:
            for group in (1, 0):
                part = slice(128 * group, 128 * group + 128)
                sent[1, part, :] = ready[part] - dependence * dot(hop_cat[1, part, :], second)
                start(1, group)
        else:
            rows = jnp.concatenate([hop_cat[1, from_slots, :], hop_cat[1, 0:64, :]], axis=0)
            sent[2, 0:128, :] = ready - dependence * dot(rows, second)
            pl.when(crosses)(last(1, me + across).start)
            pl.when(usable[0])(last(0, me + 1).start)
        image = image - dependence * dot(scatter[1], second[0:256])
        moments.append(fold(field * image))
        moments.append(fold(image * image))
        field = image
        field_cat = as_right(field)
        basis[k + 1] = field

    mapped = dot(as_left(field), var_cat[...])
    near = fold(dot(local_cat[...], field_cat) * mapped + noise * (field * field))
    high, low = split(mapped)
    picks = jnp.concatenate([gather[to_slots, :], gather[64:128, :]], axis=0)
    picked = dot(picks, high) + dot(picks, low)
    picked = (-2.0 * dependence) * picked
    lane = lax.broadcasted_iota(jnp.int32, (8, 128), 1)
    line_of = lax.broadcasted_iota(jnp.int32, (8, 128), 0)

    def pack(rows):
        tile = jnp.sum(jnp.concatenate(rows, axis=0), axis=1, keepdims=True)
        return jnp.sum(jnp.where(lane == line_of, tile, 0.0), axis=0, keepdims=True)

    early = pack(moments + [near, jnp.zeros((2, 128), F32)])
    for k in range(2):
        for c in range(4):
            pl.when(usable[c])(copy(k, c, REVERSE[c]).wait_send)
    pl.when(usable[1])(last(0, me - 1).wait_recv)
    pl.when(crossed)(last(1, me - across).wait_recv)
    cross = fold(picked * received[2, 0:128, :])
    later = sum(size - 1 for _, size in STAGES) - earlier

    @pl.when(later > 0)
    def _():
        pl.semaphore_wait(answer_sem, later)

    total = early + jnp.where(lane[0:1] == 5, total_of(cross), 0.0)

    pending = []
    for n, ((stride, size), sums) in enumerate(zip(STAGES, (sums_a, sums_b))):
        sums[0:1, :] = total
        for j, partner in partners(stride, size):
            pltpu.make_async_remote_copy(
                src_ref=sums.at[0:1, :],
                dst_ref=sums.at[j : j + 1, :],
                send_sem=sum_send_sem.at[n],
                recv_sem=sum_recv_sem.at[n],
                device_id=(partner,),
                device_id_type=MESH,
            ).start()
        whole = pltpu.make_async_remote_copy(
            src_ref=sums.at[1:size, :],
            dst_ref=sums.at[1:size, :],
            send_sem=sum_send_sem.at[n],
            recv_sem=sum_recv_sem.at[n],
            device_id=(me,),
            device_id_type=MESH,
        )
        if n == 1:
            pl.when(usable[0])(last(0, me + 1).wait_send)
            pl.when(crosses)(last(1, me + across).wait_send)
            pending[0].wait_send()
        whole.wait_recv()
        total = jnp.sum(sums[...], axis=0, keepdims=True)
        pending.append(whole)

    m = [total[:, k : k + 1] for k in range(6)]
    a0 = m[0] / m[1]
    rr1 = m[0] - 2.0 * a0 * m[1] + a0 * a0 * m[2]
    g0 = 1.0 + rr1 / m[0]
    g1 = -a0
    a1 = rr1 / (g0 * g0 * m[1] + 2.0 * g0 * g1 * m[2] + g1 * g1 * m[3])
    e1 = -a0 - a1 * g0
    e2 = -a1 * g1
    rr2 = (
        m[0] + 2.0 * e1 * m[1] + (e1 * e1 + 2.0 * e2) * m[2] + 2.0 * e1 * e2 * m[3] + e2 * e2 * m[4]
    )
    b1 = rr2 / rr1
    f0 = 1.0 + b1 * g0
    f1 = e1 + b1 * g1
    f2 = e2
    a2 = rr2 / (
        f0 * f0 * m[1]
        + 2.0 * f0 * f1 * m[2]
        + (f1 * f1 + 2.0 * f0 * f2) * m[3]
        + 2.0 * f1 * f2 * m[4]
        + f2 * f2 * m[5]
    )
    c0 = a0 + a1 * g0 + a2 * f0
    c1 = a1 * g1 + a2 * f1
    c2 = a2 * f2
    out_ref[...] = c0 * basis[0] + c1 * basis[1] + c2 * basis[2]

    pending[1].wait_send()


def local(
    right_side,
    noise_precision,
    degree,
    dependence,
    var_precision,
    local_tiles,
    tile_cols,
    tile_count,
    halo_tile,
    send_rows,
    send_count,
    halo_weights,
):
    operands = (
        right_side,
        noise_precision,
        degree.reshape(1, 256),
        dependence.reshape(1),
        var_precision,
        local_tiles,
        tile_cols,
        tile_count,
        halo_tile,
        send_rows,
        send_count,
        halo_weights,
    )
    operands = [
        x if x.size == 1 else pltpu.with_memory_space_constraint(x, pltpu.HBM) for x in operands
    ]
    specs = [pl.BlockSpec(memory_space=pltpu.SMEM if x.size == 1 else pltpu.HBM) for x in operands]
    held = (
        pltpu.VMEM((256, 256), F32),
        pltpu.VMEM((256, 256), BF16),
        pltpu.VMEM((1, 256), F32),
        pltpu.VMEM((256, 256), F32),
        pltpu.VMEM((2, 2, 128, 128), F32),
        pltpu.SMEM((2, 2), jnp.int32),
        pltpu.SMEM((2,), jnp.int32),
        pltpu.SMEM((1, 4), jnp.int32),
        pltpu.VMEM((1, 4, 64), jnp.int32),
        pltpu.SMEM((1, 4), jnp.int32),
        pltpu.VMEM((1, 4, 64, 128), F32),
    )
    return pl.pallas_call(
        kernel,
        out_shape=pltpu.VMEM((256, 256), F32),
        in_specs=specs,
        out_specs=pl.BlockSpec(memory_space=pltpu.VMEM),
        scratch_shapes=list(held)
        + [
            pltpu.VMEM((768, 256), BF16),
            pltpu.VMEM((256, 768), BF16),
            pltpu.VMEM((256, 768), BF16),
            pltpu.VMEM((2, 256, 384), BF16),
            pltpu.VMEM((2, 256, 256), BF16),
            pltpu.VMEM((256, 256), BF16),
            pltpu.VMEM((3, 256, 256), F32),
            pltpu.VMEM((3, 256, 256), F32),
            pltpu.VMEM((3, 256, 256), F32),
            pltpu.VMEM((STAGES[0][1], 128), F32),
            pltpu.VMEM((STAGES[1][1], 128), F32),
            pltpu.SemaphoreType.DMA((12,)),
            pltpu.SemaphoreType.DMA((3, 4)),
            pltpu.SemaphoreType.DMA((3, 4)),
            pltpu.SemaphoreType.DMA((2,)),
            pltpu.SemaphoreType.DMA((2,)),
            pltpu.SemaphoreType.REGULAR,
        ],
        compiler_params=pltpu.CompilerParams(
            collective_id=0, has_side_effects=True, vmem_limit_bytes=48 * 1024 * 1024
        ),
        name="conjugate_gradient",
    )(*operands)


def solution(mesh):
    placed = (
        P("dom", None),
        P("dom", None),
        P("dom"),
        P(),
        P(),
        P("dom", None, None, None),
        P("dom", None),
        P("dom"),
        P("dom", None),
        P("dom", None, None),
        P("dom", None),
        P("dom", None, None, None),
    )
    return jax.shard_map(
        local, mesh=mesh, in_specs=placed, out_specs=P("dom", None), check_vma=False
    )
```

```python
import functools

import jax
import jax.numpy as jnp
from jax import lax
from jax.experimental import pallas as pl
from jax.experimental.pallas import tpu as pltpu
from jax.sharding import PartitionSpec as P

MESH = pl.DeviceIdType.MESH
GRID_W = 16
OFFSETS = (1, -1, GRID_W, -GRID_W)
REVERSE = (1, 0, 3, 2)
STAGES = ((1, 16), (16, 32))
F32 = jnp.float32
BF16 = jnp.bfloat16


def partners_by_bit():
    groups = {}
    for mask in range(1, 16):
        groups.setdefault(1 << (mask.bit_length() - 1), []).append(mask)
    for z in range(8):
        for x in range(4):
            if z or x:
                bit = 16 << (z.bit_length() - 1) if z else 128 << (x.bit_length() - 1)
                groups.setdefault(bit, []).append(16 * z + 128 * x)
    return groups


def ring(distance, size):
    return min(distance, size - distance)


def farthest_first(stride, size):
    def hops(mask):
        if stride == 1:
            return max(ring(abs((a ^ mask) // 2 - a // 2), size // 2) for a in range(size))
        return max(
            ring(abs((a ^ mask) % 8 - a % 8), 8) + ring(abs((a ^ mask) // 8 - a // 8), size // 8)
            for a in range(size)
        )

    return sorted(range(1, size), key=lambda mask: -hops(mask))


def split(value):
    high = value.astype(BF16)
    low = (value - high.astype(F32)).astype(BF16)
    return high, low


def as_left(value):
    high, low = split(value)
    return jnp.concatenate([high, low, high], axis=1)


def as_right(value):
    high, low = split(value)
    return jnp.concatenate([high, low, high], axis=0)


def keep_left(ref, value):
    high, low = split(value)
    n = value.shape[1]
    ref[:, 0:n] = high
    ref[:, n : 2 * n] = high
    ref[:, 2 * n : 3 * n] = low


def keep_right(ref, value):
    high, low = split(value)
    n = value.shape[0]
    ref[0:n, :] = high
    ref[n : 2 * n, :] = high
    ref[2 * n : 3 * n, :] = low


def dot(a, b):
    return jnp.dot(a, b, preferred_element_type=F32)


def fold(value):
    rows, lanes = value.shape
    tile = jnp.sum(value.reshape(rows // 8, 8, lanes), axis=0)
    tile = tile[:, 0:128] + tile[:, 128:256]
    return jnp.sum(tile, axis=0, keepdims=True)


def total_of(row):
    return jnp.sum(row, axis=1, keepdims=True)


def kernel(
    right_hbm,
    noise_hbm,
    degree_hbm,
    dependence_ref,
    var_hbm,
    tiles_hbm,
    cols_hbm,
    count_hbm,
    border_hbm,
    rows_hbm,
    live_hbm,
    halo_hbm,
    out_ref,
    right_ref,
    noise_ref,
    degree_ref,
    var_ref,
    tiles_ref,
    cols_ref,
    count_ref,
    border_ref,
    rows_ref,
    live_ref,
    halo_ref,
    var_cat,
    local_cat,
    halo_cat,
    hop_cat,
    scatter,
    gather,
    basis,
    sent,
    received,
    sums_a,
    sums_b,
    load_sem,
    send_sem,
    recv_sem,
    sum_send_sem,
    sum_recv_sem,
    answer_sem,
):
    me = lax.axis_index("dom")
    pairs = {
        "right": (right_hbm.at[0:128, :], right_ref.at[0:128, :]),
        "right_too": (right_hbm.at[128:256, :], right_ref.at[128:256, :]),
        "noise": (noise_hbm, noise_ref),
        "degree": (degree_hbm, degree_ref),
        "var": (var_hbm, var_ref),
        "tiles": (tiles_hbm, tiles_ref),
        "cols": (cols_hbm, cols_ref),
        "count": (count_hbm, count_ref),
        "border": (border_hbm, border_ref),
        "rows": (rows_hbm, rows_ref),
        "live": (live_hbm, live_ref),
        "halo": (halo_hbm, halo_ref),
    }
    loads = {
        name: pltpu.make_async_copy(src, dst, load_sem.at[i])
        for i, (name, (src, dst)) in enumerate(pairs.items())
    }
    for name in ("right", "right_too", "halo", "border"):
        loads[name].start()

    column = jnp.bitwise_and(me, GRID_W - 1)
    line = jnp.right_shift(me, 4)
    usable = (column < GRID_W - 1, column > 0, line < 512 // GRID_W - 1, line > 0)

    odd = jnp.bitwise_and(me, 1)

    def partners(stride, size):
        return [(j, jnp.bitwise_xor(me, j * stride)) for j in farthest_first(stride, size)]

    barrier = pltpu.get_barrier_semaphore()
    for c in range(4):

        @pl.when(usable[c])
        def _():
            pl.semaphore_signal(barrier, inc=1, device_id=(me + OFFSETS[c],), device_id_type=MESH)

    for bit, masks in partners_by_bit().items():

        @pl.when(jnp.bitwise_and(me, bit) == 0)
        def _():
            for mask in masks:
                greet = jnp.bitwise_xor(me, mask)
                pl.semaphore_signal(barrier, inc=1, device_id=(greet,), device_id_type=MESH)

    earlier = column + 4 * jnp.bitwise_and(line, 7) + jnp.right_shift(me, 7)

    for name in ("var", "live", "rows", "tiles", "cols", "count", "degree", "noise"):
        loads[name].start()

    def copy(k, c, to):
        return pltpu.make_async_remote_copy(
            src_ref=sent.at[k, 64 * c : 64 * c + 64, :],
            dst_ref=received.at[k, 64 * to : 64 * to + 64, :],
            send_sem=send_sem.at[k, c],
            recv_sem=recv_sem.at[k, to],
            device_id=(me + OFFSETS[c],),
            device_id_type=MESH,
        )

    groups = ((0, 1), (2, 3))

    def start(k, group):
        for c in groups[group]:
            pl.when(usable[c])(copy(k, c, REVERSE[c]).start)

    def finish(k, group):
        for c in groups[group]:
            pl.when(usable[c])(copy(k, c, c).wait_recv)

    def last(i, device):
        i = 1 - i
        return pltpu.make_async_remote_copy(
            src_ref=sent.at[2, 64 * i : 64 * i + 64, :],
            dst_ref=received.at[2, 64 * i : 64 * i + 64, :],
            send_sem=send_sem.at[2, i],
            recv_sem=recv_sem.at[2, i],
            device_id=(device,),
            device_id_type=MESH,
        )

    across = GRID_W * (1 - 2 * odd)
    down, up = usable[3], usable[2]
    even = odd == 0
    crosses = jnp.logical_or(jnp.logical_and(even, up), jnp.logical_and(odd == 1, down))
    crossed = jnp.logical_or(jnp.logical_and(even, down), jnp.logical_and(odd == 1, up))
    from_slots = pl.ds(pl.multiple_of(128 + 64 * odd, 64), 64)
    to_slots = pl.ds(pl.multiple_of(192 - 64 * odd, 64), 64)

    @pl.when(jnp.logical_not(usable[1]))
    def _():
        received[2, 64:128, :] = jnp.zeros((64, 256), F32)

    @pl.when(jnp.logical_not(crossed))
    def _():
        received[2, 0:64, :] = jnp.zeros((64, 256), F32)

    loads["border"].wait()
    loads["halo"].wait()
    loads["right"].wait()
    loads["right_too"].wait()
    field = right_ref[...]
    field_cat = as_right(field)
    for group in (1, 0):
        for c in groups[group]:
            tile = border_ref[0, c]
            weights = halo_ref[0, c]
            block = jnp.concatenate(
                [jnp.where(tile == r, weights, jnp.zeros_like(weights)) for r in range(2)], axis=1
            )
            keep_left(halo_cat.at[64 * c : 64 * c + 64, :], block)
        part = slice(128 * group, 128 * group + 128)
        sent[0, part, :] = dot(halo_cat[part, :], field_cat)
        if group:
            pl.semaphore_wait(barrier, earlier + sum(u.astype(jnp.int32) for u in usable))
        start(0, group)

    for c in range(4):

        @pl.when(jnp.logical_not(usable[c]))
        def _():
            for k in range(2):
                received[k, 64 * c : 64 * c + 64, :] = jnp.zeros((64, 256), F32)

    loads["var"].wait()
    keep_right(var_cat, var_ref[...])

    loads["live"].wait()
    loads["rows"].wait()
    places = []
    slot = lax.broadcasted_iota(jnp.int32, (1, 64), 1)
    for c in range(4):
        place = rows_ref[0, c : c + 1, :] + border_ref[0, c] * 128
        places.append(jnp.where(slot < live_ref[0, c], place, -1))
    places = jnp.concatenate(places, axis=1)
    hot = lax.broadcasted_iota(jnp.int32, (256, 256), 0) == places
    hot_wide = jnp.where(hot, 1.0, 0.0)
    hot = hot_wide.astype(BF16)
    for group in range(2):
        scatter[group, :, 0:128] = hot[:, 128 * group : 128 * group + 128]
        scatter[group, :, 128:256] = hot[:, 128 * group : 128 * group + 128]

    for name in ("tiles", "cols", "count", "degree"):
        loads[name].wait()
    dependence = dependence_ref[0]
    on_diagonal = lax.broadcasted_iota(jnp.int32, (256, 256), 0) == lax.broadcasted_iota(
        jnp.int32, (256, 256), 1
    )
    diagonal = jnp.where(on_diagonal, degree_ref[...], 0.0)
    for r in range(2):
        row = []
        for s in range(2):
            block = jnp.zeros((128, 128), F32)
            for j in range(2):
                used = jnp.logical_and(cols_ref[r, j] == s, count_ref[r] > j)
                block = jnp.where(used, tiles_ref[r, j], block)
            row.append(block)
        block_row = diagonal[128 * r : 128 * r + 128] - dependence * jnp.concatenate(row, axis=1)
        keep_left(local_cat.at[128 * r : 128 * r + 128, :], block_row)
    loads["noise"].wait()
    noise = noise_ref[...].astype(F32)

    hop_high = dot(halo_cat[:, 0:256], hot).astype(BF16)
    hop_low = dot(halo_cat[:, 512:768], hot).astype(BF16)
    for group in range(2):
        part = slice(128 * group, 128 * group + 128)
        hop_cat[group, :, 0:128] = hop_high[:, part]
        hop_cat[group, :, 128:256] = hop_high[:, part]
        hop_cat[group, :, 256:384] = hop_low[:, part]
    gather[...] = hot_wide.T.astype(BF16)

    for bit, masks in partners_by_bit().items():

        @pl.when(jnp.bitwise_and(me, bit) != 0)
        def _():
            for mask in masks:
                answer = jnp.bitwise_xor(me, mask)
                pl.semaphore_signal(answer_sem, inc=1, device_id=(answer,), device_id_type=MESH)


    basis[0] = field
    moments = [fold(field * field)]
    for k in range(2):
        near = dot(as_left(dot(local_cat[...], field_cat)), var_cat[...]) + noise * field
        next_near = dot(halo_cat[...], as_right(near))
        finish(k, 0)
        first = as_right(dot(as_left(received[k, 0:128, :]), var_cat[...]))
        image = near - dependence * dot(scatter[0], first[0:256])
        if k == 0:
            ready = next_near - dependence * dot(hop_cat[0], first)
        else:
            rows = jnp.concatenate([hop_cat[0, from_slots, :], hop_cat[0, 0:64, :]], axis=0)
            crossing = jnp.where(even, next_near[128:192], next_near[192:256])
            ready = jnp.concatenate([crossing, next_near[0:64]], axis=0)
            ready = ready - dependence * dot(rows, first)
        finish(k, 1)
        second = as_right(dot(as_left(received[k, 128:256, :]), var_cat[...]))
        if k == 0:
            for group in (1, 0):
                part = slice(128 * group, 128 * group + 128)
                sent[1, part, :] = ready[part] - dependence * dot(hop_cat[1, part, :], second)
                start(1, group)
        else:
            rows = jnp.concatenate([hop_cat[1, from_slots, :], hop_cat[1, 0:64, :]], axis=0)
            sent[2, 0:128, :] = ready - dependence * dot(rows, second)
            pl.when(crosses)(last(1, me + across).start)
            pl.when(usable[0])(last(0, me + 1).start)
        image = image - dependence * dot(scatter[1], second[0:256])
        moments.append(fold(field * image))
        moments.append(fold(image * image))
        field = image
        field_cat = as_right(field)
        basis[k + 1] = field

    mapped = dot(as_left(field), var_cat[...])
    near = fold(dot(local_cat[...], field_cat) * mapped + noise * (field * field))
    high, low = split(mapped)
    picks = jnp.concatenate([gather[to_slots, :], gather[64:128, :]], axis=0)
    picked = dot(picks, high) + dot(picks, low)
    picked = (-2.0 * dependence) * picked
    lane = lax.broadcasted_iota(jnp.int32, (8, 128), 1)
    line_of = lax.broadcasted_iota(jnp.int32, (8, 128), 0)

    def pack(rows):
        tile = jnp.sum(jnp.concatenate(rows, axis=0), axis=1, keepdims=True)
        return jnp.sum(jnp.where(lane == line_of, tile, 0.0), axis=0, keepdims=True)

    early = pack(moments + [near, jnp.zeros((2, 128), F32)])
    for k in range(2):
        for c in range(4):
            pl.when(usable[c])(copy(k, c, REVERSE[c]).wait_send)
    pl.when(usable[1])(last(0, me - 1).wait_recv)
    pl.when(crossed)(last(1, me - across).wait_recv)
    cross = fold(picked * received[2, 0:128, :])
    later = sum(size - 1 for _, size in STAGES) - earlier

    @pl.when(later > 0)
    def _():
        pl.semaphore_wait(answer_sem, later)

    total = early + jnp.where(lane[0:1] == 5, total_of(cross), 0.0)

    pending = []
    for n, ((stride, size), sums) in enumerate(zip(STAGES, (sums_a, sums_b))):
        sums[0:1, :] = total
        for j, partner in partners(stride, size):
            pltpu.make_async_remote_copy(
                src_ref=sums.at[0:1, :],
                dst_ref=sums.at[j : j + 1, :],
                send_sem=sum_send_sem.at[n],
                recv_sem=sum_recv_sem.at[n],
                device_id=(partner,),
                device_id_type=MESH,
            ).start()
        whole = pltpu.make_async_remote_copy(
            src_ref=sums.at[1:size, :],
            dst_ref=sums.at[1:size, :],
            send_sem=sum_send_sem.at[n],
            recv_sem=sum_recv_sem.at[n],
            device_id=(me,),
            device_id_type=MESH,
        )
        if n == 1:
            pl.when(usable[0])(last(0, me + 1).wait_send)
            pl.when(crosses)(last(1, me + across).wait_send)
            pending[0].wait_send()
        whole.wait_recv()
        total = jnp.sum(sums[...], axis=0, keepdims=True)
        pending.append(whole)

    m = [total[:, k : k + 1] for k in range(6)]
    a0 = m[0] / m[1]
    rr1 = m[0] - 2.0 * a0 * m[1] + a0 * a0 * m[2]
    g0 = 1.0 + rr1 / m[0]
    g1 = -a0
    a1 = rr1 / (g0 * g0 * m[1] + 2.0 * g0 * g1 * m[2] + g1 * g1 * m[3])
    e1 = -a0 - a1 * g0
    e2 = -a1 * g1
    rr2 = (
        m[0] + 2.0 * e1 * m[1] + (e1 * e1 + 2.0 * e2) * m[2] + 2.0 * e1 * e2 * m[3] + e2 * e2 * m[4]
    )
    b1 = rr2 / rr1
    f0 = 1.0 + b1 * g0
    f1 = e1 + b1 * g1
    f2 = e2
    a2 = rr2 / (
        f0 * f0 * m[1]
        + 2.0 * f0 * f1 * m[2]
        + (f1 * f1 + 2.0 * f0 * f2) * m[3]
        + 2.0 * f1 * f2 * m[4]
        + f2 * f2 * m[5]
    )
    c0 = a0 + a1 * g0 + a2 * f0
    c1 = a1 * g1 + a2 * f1
    c2 = a2 * f2
    out_ref[...] = c0 * basis[0] + c1 * basis[1] + c2 * basis[2]

    pending[1].wait_send()


def local(
    right_side,
    noise_precision,
    degree,
    dependence,
    var_precision,
    local_tiles,
    tile_cols,
    tile_count,
    halo_tile,
    send_rows,
    send_count,
    halo_weights,
):
    operands = (
        right_side,
        noise_precision,
        degree.reshape(1, 256),
        dependence.reshape(1),
        var_precision,
        local_tiles,
        tile_cols,
        tile_count,
        halo_tile,
        send_rows,
        send_count,
        halo_weights,
    )
    operands = [
        x if x.size == 1 else pltpu.with_memory_space_constraint(x, pltpu.HBM) for x in operands
    ]
    specs = [pl.BlockSpec(memory_space=pltpu.SMEM if x.size == 1 else pltpu.HBM) for x in operands]
    held = (
        pltpu.VMEM((256, 256), F32),
        pltpu.VMEM((256, 256), BF16),
        pltpu.VMEM((1, 256), F32),
        pltpu.VMEM((256, 256), F32),
        pltpu.VMEM((2, 2, 128, 128), F32),
        pltpu.SMEM((2, 2), jnp.int32),
        pltpu.SMEM((2,), jnp.int32),
        pltpu.SMEM((1, 4), jnp.int32),
        pltpu.VMEM((1, 4, 64), jnp.int32),
        pltpu.SMEM((1, 4), jnp.int32),
        pltpu.VMEM((1, 4, 64, 128), F32),
    )
    return pl.pallas_call(
        kernel,
        out_shape=pltpu.VMEM((256, 256), F32),
        in_specs=specs,
        out_specs=pl.BlockSpec(memory_space=pltpu.VMEM),
        scratch_shapes=list(held)
        + [
            pltpu.VMEM((768, 256), BF16),
            pltpu.VMEM((256, 768), BF16),
            pltpu.VMEM((256, 768), BF16),
            pltpu.VMEM((2, 256, 384), BF16),
            pltpu.VMEM((2, 256, 256), BF16),
            pltpu.VMEM((256, 256), BF16),
            pltpu.VMEM((3, 256, 256), F32),
            pltpu.VMEM((3, 256, 256), F32),
            pltpu.VMEM((3, 256, 256), F32),
            pltpu.VMEM((STAGES[0][1], 128), F32),
            pltpu.VMEM((STAGES[1][1], 128), F32),
            pltpu.SemaphoreType.DMA((12,)),
            pltpu.SemaphoreType.DMA((3, 4)),
            pltpu.SemaphoreType.DMA((3, 4)),
            pltpu.SemaphoreType.DMA((2,)),
            pltpu.SemaphoreType.DMA((2,)),
            pltpu.SemaphoreType.REGULAR,
        ],
        compiler_params=pltpu.CompilerParams(
            collective_id=0, has_side_effects=True, vmem_limit_bytes=48 * 1024 * 1024
        ),
        name="conjugate_gradient",
    )(*operands)


def solution(mesh):
    placed = (
        P("dom", None),
        P("dom", None),
        P("dom"),
        P(),
        P(),
        P("dom", None, None, None),
        P("dom", None),
        P("dom"),
        P("dom", None),
        P("dom", None, None),
        P("dom", None),
        P("dom", None, None, None),
    )
    return jax.shard_map(
        local, mesh=mesh, in_specs=placed, out_specs=P("dom", None), check_vma=False
    )
```
